256 devices in a mesh: dt: 16 (over x, y_hi, core), ch: 16 (over y_lo, z).
Axes of the slice: x: 4, y: 4 (y_hi: 2, y_lo: 2; y = y_hi * 2 + y_lo), z: 8, core: 2. Of those that a mesh axis runs over, the one named last changes fastest.
Arguments:
- inputs: bfloat16 [640, 16, 2304], P('ch', 'dt'), may hold values from -24 to 24, as said below
- spatial_weight: bfloat16 [9, 640, 640], P(None, 'ch', 'dt'), may hold values from -0.6 to 0.6, as said below
- temporal_weight: bfloat16 [3, 640, 640], P(None, 'ch', 'dt'), may hold values from -0.125 to 0.125
- norm_gain: float32 [640], P('ch'), may hold values from 0.1 to 1.9
- norm_bias: float32 [640], P('ch'), may hold values from -4 to 4
- cotangent: bfloat16 [640, 16, 2304], P('ch', 'dt'), may hold values from -6 to 6
Outputs:
- output: bfloat16 [640, 16, 2304], P('ch', 'dt')
- grad_inputs: bfloat16 [640, 16, 2304], P('ch', 'dt')
- grad_spatial: float32 [9, 640, 640], P(None, 'ch', 'dt')
- grad_temporal: float32 [3, 640, 640], P(None, 'ch', 'dt')
- grad_gain: float32 [640], P('ch')
- grad_bias: float32 [640], P('ch')
The draws below stay inside these ranges and needn't reach their ends.
Inputs may be any that keep to these rules, and one draw needn't show every extreme that they name: `inputs`: Real-valued activations with independent entries; their magnitude varies by frame and by channel. `spatial_weight`: Real-valued weights with independent entries; their magnitude varies by output channel.
All inputs are finite; a program needn't handle non-finite values.
Results may differ from the reference program's by a relative error of at most 0.0046.
Values may be sent and summed in bfloat16 or wider, within the bound.
No kernel may reach another device: no remote copies, remote signals or barrier semaphores. Data moves between devices by JAX's collectives and lax.ppermute only.
A program may use at most 64 MiB of HBM per device.

```python
import jax
import jax.numpy as jnp
from jax import lax

C = 640
G = 32
H = 36
W = 64
FRAMES = 16


def draw_inputs(key, part):
    key = jax.random.fold_in(key, 11)
    first_key, second_key = jax.random.split(key)
    shape = (C, FRAMES, H * W)
    base = jnp.clip(jax.random.normal(first_key, shape, jnp.float32), -4.0, 4.0)
    frame_scale = 1.0 + 2.0 * jnp.arange(FRAMES, dtype=jnp.float32) / (FRAMES - 1)
    channel_scale = jnp.exp(jax.random.uniform(second_key, (C,), jnp.float32, jnp.log(0.5), jnp.log(2.0)))
    return (base * frame_scale[None, :, None] * channel_scale[:, None, None]).astype(jnp.bfloat16)


def draw_spatial_weight(key, part):
    key = jax.random.fold_in(key, 12)
    first_key, second_key = jax.random.split(key)
    shape = (9, C, C)
    base = jnp.clip(jax.random.normal(first_key, shape, jnp.float32), -4.0, 4.0)
    column_scale = jnp.exp(jax.random.uniform(second_key, (C,), jnp.float32, jnp.log(0.3), jnp.log(3.0)))
    return (base * (9.0 * C) ** (-0.5) * column_scale[None, None, :]).astype(jnp.bfloat16)


def spiked(values, own_key, source, target, blocks, factor):
    owner, partner = [(jnp.arange(values.shape[position]) // (values.shape[position] // blocks)).reshape([-1 if axis == position else 1 for axis in range(values.ndim)]) for position in (source, target)]
    chosen = jax.random.permutation(own_key, blocks)[partner]
    strong = (owner == chosen) | (owner == (partner + blocks // 2) % blocks)
    return jnp.where(strong, factor * values, values)


def shard_levels(rng, dims, cuts, smallest, largest):
    level = 1.0
    for position, shards_of in cuts:
        heights = jax.random.uniform(jax.random.fold_in(jax.random.fold_in(rng, 6), position), (shards_of,), jnp.float32, smallest / len(cuts), largest / len(cuts))
        level = level * jnp.repeat(jnp.exp(heights), dims[position] // shards_of).reshape((-1,) + (1,) * (len(dims) - 1 - position))
    return level


def noise(stream_key, extent, scale, most, cuts=(), kind=jnp.bfloat16):
    array = jax.random.normal(stream_key, extent, jnp.float32) * scale
    if len(cuts) > 0:
        array = shard_levels(stream_key, extent, cuts, -0.22, 0.18) * array
    return jnp.clip(array, min=-most, max=most).astype(kind)


def heavy_noise(key, shape, scale, most, cuts, heavy, kind=jnp.bfloat16):
    result = scale * jax.random.normal(key, shape, jnp.float32)
    if cuts:
        result = result * shard_levels(key, shape, cuts, -0.22, 0.18)
    return jnp.clip(spiked(result, jax.random.fold_in(key, 3), *heavy), -most, most).astype(kind)


def setup_inputs(seed: int = 0) -> dict:
    streams_of = jax.random.split(jax.random.key(seed), 7)
    inputs = draw_inputs(jax.random.fold_in(streams_of[6], 71), 0)
    spatial_weight = draw_spatial_weight(jax.random.fold_in(streams_of[6], 71), 0)
    temporal_weight = noise(streams_of[2], (3, C, C), (3 * C) ** -0.5, 0.125, ((1, 16), (2, 16)))
    norm_gain = jnp.clip(1.0 + 0.18 * jax.random.normal(streams_of[3], (C,), jnp.float32), 0.1, 1.9)
    norm_bias = noise(streams_of[4], (C,), 1.0, 4.0, ((0, 16),), jnp.float32)
    cotangent = heavy_noise(streams_of[5], (C, FRAMES, H * W), 1.0, 6.0, ((0, 16), (1, 16)), (1, 0, 16, 2.0))
    return {"inputs": inputs, "spatial_weight": spatial_weight, "temporal_weight": temporal_weight, "norm_gain": norm_gain, "norm_bias": norm_bias, "cotangent": cotangent}


TAP_STEPS = ((-1, -1), (-1, 0), (-1, 1), (0, -1), (0, 0), (0, 1), (1, -1), (1, 0), (1, 1))

def shift_cells(field, row_step, col_step, row_width):
    cell_count = field.shape[-1]
    margin = row_width + 1
    padding = [(0, 0)] * (field.ndim - 1) + [(margin, margin)]
    padded = jnp.pad(field, padding)
    begin_at = margin + row_step * row_width + col_step
    shifted = lax.slice_in_dim(padded, begin_at, begin_at + cell_count, axis=field.ndim - 1)
    column = jnp.arange(cell_count, dtype=jnp.int32) % row_width
    inside = (column + col_step >= 0) & (column + col_step < row_width)
    return jnp.where(inside, shifted, jnp.zeros((), field.dtype))

def tap_stack(field, row_width, direction):
    return jnp.stack([shift_cells(field, direction * tap_step[0], direction * tap_step[1], row_width) for tap_step in TAP_STEPS])

def reference(inputs, spatial_weight, temporal_weight, norm_gain, norm_bias, cotangent):
    channels, frame_count, cell_count = inputs.shape
    group_width = C // G
    members = group_width * frame_count * cell_count
    weight_wide = spatial_weight.astype(jnp.float32)
    temporal_wide = temporal_weight.astype(jnp.float32)

    def conv_frame(frame_cells):
        shifted = tap_stack(frame_cells, W, 1).astype(jnp.float32)
        return jnp.einsum('tio,tip->op', weight_wide, shifted)
    by_frame = jnp.moveaxis(inputs, 1, 0)
    conv_out = jnp.moveaxis(lax.map(conv_frame, by_frame), 0, 1).astype(jnp.bfloat16)
    grouped = conv_out.astype(jnp.float32).reshape(G, group_width, frame_count, cell_count)
    sums = lax.optimization_barrier(jnp.sum(grouped, axis=(1, 2, 3)))
    squares = lax.optimization_barrier(jnp.sum(grouped * grouped, axis=(1, 2, 3)))
    center = sums / members
    variance = squares / members - center * center
    inverse = lax.rsqrt(variance + 1e-05)
    normed_grouped = (grouped - center[:, None, None, None]) * inverse[:, None, None, None]
    normed = normed_grouped.reshape(channels, frame_count, cell_count)
    affine = normed * norm_gain[:, None, None] + norm_bias[:, None, None]
    activated = jax.nn.silu(affine).astype(jnp.bfloat16)
    rimmed = jnp.pad(activated, ((0, 0), (1, 1), (0, 0))).astype(jnp.float32)
    mixed = jnp.zeros((channels, frame_count, cell_count), jnp.float32)
    for which in range(3):
        mixed = mixed + jnp.einsum('io,ifp->ofp', temporal_wide[which], rimmed[:, which:which + frame_count])
    output = (inputs.astype(jnp.float32) + mixed).astype(jnp.bfloat16)
    upstream = cotangent.astype(jnp.float32)
    grad_temporal = jnp.stack([jnp.einsum('ifp,ofp->io', rimmed[:, which:which + frame_count], upstream) for which in range(3)])
    up_padded = jnp.pad(upstream, ((0, 0), (1, 1), (0, 0)))
    grad_act = jnp.zeros((channels, frame_count, cell_count), jnp.float32)
    for which in range(3):
        grad_act = grad_act + jnp.einsum('io,ofp->ifp', temporal_wide[which], up_padded[:, 2 - which:2 - which + frame_count])
    sigmoid = jax.nn.sigmoid(affine)
    grad_affine = grad_act * sigmoid * (1.0 + affine * (1.0 - sigmoid))
    grad_gain = lax.optimization_barrier(jnp.sum(grad_affine * normed, axis=(1, 2)))
    grad_bias = lax.optimization_barrier(jnp.sum(grad_affine, axis=(1, 2)))
    grad_normed = (grad_affine * norm_gain[:, None, None]).reshape(G, group_width, frame_count, cell_count)
    first_mean = lax.optimization_barrier(jnp.sum(grad_normed, axis=(1, 2, 3))) / members
    second_mean = lax.optimization_barrier(jnp.sum(grad_normed * normed_grouped, axis=(1, 2, 3))) / members
    grad_conv = inverse[:, None, None, None] * (grad_normed - first_mean[:, None, None, None] - normed_grouped * second_mean[:, None, None, None])
    grad_conv = grad_conv.reshape(channels, frame_count, cell_count).astype(jnp.bfloat16)

    def back_frame(carry, frame_pair):
        frame_cells, frame_grad = frame_pair
        shifted = tap_stack(frame_cells, W, 1).astype(jnp.float32)
        grad_wide = frame_grad.astype(jnp.float32)
        carry = carry + jnp.einsum('tip,op->tio', shifted, grad_wide)
        spread_back = jnp.einsum('tio,op->tip', weight_wide, grad_wide)
        returned = jnp.zeros((channels, cell_count), jnp.float32)
        for which in range(9):
            tap_step = TAP_STEPS[which]
            returned = returned + shift_cells(spread_back[which], -tap_step[0], -tap_step[1], W)
        return (carry, returned)
    grad_spatial, conv_back = lax.scan(back_frame, jnp.zeros((9, channels, channels), jnp.float32), (by_frame, jnp.moveaxis(grad_conv, 1, 0)))
    conv_back = jnp.moveaxis(conv_back, 0, 1)
    grad_inputs = (upstream + conv_back).astype(jnp.bfloat16)
    return (output, grad_inputs, grad_spatial, grad_temporal, grad_gain, grad_bias)
```

```python
import jax
import jax.numpy as jnp
from jax import lax
from jax.experimental import pallas as pl
from jax.experimental.pallas import tpu as pltpu
from jax.sharding import PartitionSpec as P

C = 640
G = 32
W = 64
CELLS = 2304
FRAMES = 16
BLK = 40
MEMBERS = (C // G) * FRAMES * CELLS
TAPS = ((-1, -1), (-1, 0), (-1, 1), (0, -1), (0, 0), (0, 1), (1, -1), (1, 0), (1, 1))
SP = 384
TP = 128
BF = jnp.bfloat16
F32 = jnp.float32


def split(block):
    return (block >> 1) & 3, ((block >> 3) << 1) | (block & 1)


def join(a, b):
    return ((b >> 1) << 3) | (a << 1) | (b & 1)


def over_a(value, k):
    return lax.ppermute(value, "ch", [(i, i ^ (k << 1)) for i in range(16)])


def over_b(value, l):
    mask = join(0, l)
    return lax.ppermute(value, "ch", [(i, i ^ mask) for i in range(16)])


def piece_moves():
    moves = []
    for into in range(16):
        for out in range(16):
            (a, b), (c, d) = split(into), split(out)
            place = ((a ^ c) * 4 + (b ^ d)) * 16 + join(c, b)
            moves.append((out * 16 + into, place))
    return moves


def neighbours(value):
    before = lax.ppermute(value, "dt", [(i, i + 1) for i in range(15)])
    after = lax.ppermute(value, "dt", [(i + 1, i) for i in range(15)])
    return before, after


def params(limit=50):
    return pltpu.CompilerParams(vmem_limit_bytes=limit * 1024 * 1024)


def shape(dims, dtype):
    return jax.ShapeDtypeStruct(dims, dtype)


def shifted(value, row_step, col_step):
    cell = lax.broadcasted_iota(jnp.int32, (1, CELLS), 1)
    col = cell & (W - 1)
    inside = jnp.ones((1, CELLS), F32)
    if row_step == -1:
        inside = jnp.where(cell >= W, inside, 0.0)
    if row_step == 1:
        inside = jnp.where(cell < CELLS - W, inside, 0.0)
    if col_step == -1:
        inside = jnp.where(col >= 1, inside, 0.0)
    if col_step == 1:
        inside = jnp.where(col < W - 1, inside, 0.0)
    step = row_step * W + col_step
    if step == 0:
        return value
    return pltpu.roll(value, (-step) % CELLS, 1) * inside


def fill_taps(taps_ref, base, value, direction):
    wide = value.astype(F32)
    held = []
    for t, (a, b) in enumerate(TAPS):
        held.append(shifted(wide, direction * a, direction * b))
        if len(held) == 2:
            taps_ref[pl.ds(base + (t - 1) * BLK, 2 * BLK), :] = jnp.concatenate(held, 0).astype(BF)
            held = []
    held.append(jnp.zeros((SP - 9 * BLK, CELLS), F32))
    taps_ref[pl.ds(base + 8 * BLK, SP - 8 * BLK), :] = jnp.concatenate(held, 0).astype(BF)


def left_matrix(weights_ref, side, first, width, stride_row, stride_col):
    rows = []
    for r in range(4):
        parts = [
            weights_ref[r * stride_row + c * stride_col, side, :, first : first + width].astype(F32)
            for c in range(4)
        ]
        rows.append(jnp.concatenate(parts, 1))
    return jnp.concatenate(rows, 0).astype(BF)


def spread(left, right_ref, own_ref, send_refs):
    width = 256

    def chunk(c, carry):
        cols = pl.ds(pl.multiple_of(c * width, width), width)
        part = jnp.dot(left, right_ref[:, cols], preferred_element_type=F32)
        own_ref[:, cols] = part[:BLK]
        for n, ref in enumerate(send_refs):
            ref[:, cols] = part[(n + 1) * BLK : (n + 2) * BLK].astype(BF)
        return carry

    lax.fori_loop(0, CELLS // width, chunk, 0)


PARTIALS = [shape((BLK, CELLS), F32)] + [shape((BLK, CELLS), BF)] * 3


def conv_kernel(x0, x1, x2, x3, weights, own, s1, s2, s3, taps):
    for k, ref in enumerate((x0, x1, x2, x3)):
        fill_taps(taps, k * SP, ref[...], 1)
    left = left_matrix(weights, 1, 0, SP, 1, 4)
    spread(left, taps, own, (s1, s2, s3))


def conv_forward(xs, weights):
    return pl.pallas_call(
        conv_kernel,
        out_shape=PARTIALS,
        scratch_shapes=[pltpu.VMEM((4 * SP, CELLS), BF)],
        compiler_params=params(),
        name="conv_forward",
    )(*xs, weights)


def back_kernel(g0, g1, g2, g3, x0, x1, x2, x3, weights, own, s1, s2, s3, grad, taps):
    for l, ref in enumerate((g0, g1, g2, g3)):
        fill_taps(taps, l * SP, ref[...], -1)
    left = left_matrix(weights, 0, 0, SP, 4, 1)
    spread(left, taps, own, (s1, s2, s3))
    field = jnp.concatenate([ref[...].astype(F32) for ref in (x0, x1, x2, x3)], 0).astype(BF)
    for l in range(4):
        part = lax.dot_general(
            field, taps[l * SP : (l + 1) * SP, :], (((1,), (1,)), ((), ())), preferred_element_type=F32
        )
        for k in range(4):
            grad[k * 4 + l] = part[k * BLK : (k + 1) * BLK]


def conv_backward(gs, xs, weights):
    return pl.pallas_call(
        back_kernel,
        out_shape=PARTIALS + [shape((16, BLK, SP), F32)],
        scratch_shapes=[pltpu.VMEM((4 * SP, CELLS), BF)],
        compiler_params=params(),
        name="conv_backward",
    )(*gs, *xs, weights)


def fill_frames(stack_ref, first, second, third):
    for n in range(4):
        parts = [ref[n].astype(F32) for ref in (first, second, third)]
        parts.append(jnp.zeros((TP - 3 * BLK, CELLS), F32))
        stack_ref[n * TP : (n + 1) * TP, :] = jnp.concatenate(parts, 0).astype(BF)


def time_kernel(side, strides, first, second, third, weights, own, s1, s2, s3, stack):
    fill_frames(stack, first, second, third)
    left = left_matrix(weights, side, SP, TP, *strides)
    spread(left, stack, own, (s1, s2, s3))


def time_mix(frames, weights, side):
    strides = (4, 1) if side == 0 else (1, 4)

    def kernel(*refs):
        time_kernel(side, strides, *refs)

    return pl.pallas_call(
        kernel,
        out_shape=PARTIALS,
        scratch_shapes=[pltpu.VMEM((4 * TP, CELLS), BF)],
        compiler_params=params(),
        name="time_mix",
    )(*frames, weights)


def time_grad_kernel(act, first, second, third, grad, stack):
    fill_frames(stack, first, second, third)
    field = jnp.concatenate([act[k].astype(F32) for k in range(4)], 0).astype(BF)
    part = lax.dot_general(field, stack[...], (((1,), (1,)), ((), ())), preferred_element_type=F32)
    for k in range(4):
        for l in range(4):
            grad[k * 4 + l] = part[k * BLK : (k + 1) * BLK, l * TP : (l + 1) * TP]


def time_grad(act4, frames):
    return pl.pallas_call(
        time_grad_kernel,
        out_shape=shape((16, BLK, TP), F32),
        scratch_shapes=[pltpu.VMEM((4 * TP, CELLS), BF)],
        compiler_params=params(),
        name="time_grad",
    )(act4, *frames)


def lane_rows():
    return (
        lax.broadcasted_iota(jnp.int32, (BLK, 128), 0),
        lax.broadcasted_iota(jnp.int32, (BLK, 128), 1),
    )


def to_lanes(low, high):
    row, lane = lane_rows()
    both = jnp.where(lane == row, low, 0.0) + jnp.where(lane == row + 64, high, 0.0)
    return jnp.broadcast_to(jnp.sum(both, axis=0, keepdims=True), (16, 128))


def column(row_ref):
    row = lax.broadcasted_iota(jnp.int32, (BLK, BLK), 0)
    lane = lax.broadcasted_iota(jnp.int32, (BLK, BLK), 1)
    return jnp.sum(jnp.where(row == lane, row_ref[...], 0.0), axis=1, keepdims=True)


def group_stats(sums_ref):
    row, lane = lane_rows()
    total = jnp.sum(sums_ref[...], axis=0, keepdims=True)
    upper = row >= BLK // 2
    low = (lane < BLK) & ((lane >= BLK // 2) == upper)
    high = (lane >= 64) & (lane < 64 + BLK) & ((lane >= 64 + BLK // 2) == upper)
    center = jnp.sum(jnp.where(low, total, 0.0), axis=1, keepdims=True) / MEMBERS
    squares = jnp.sum(jnp.where(high, total, 0.0), axis=1, keepdims=True) / MEMBERS
    return center, lax.rsqrt(squares - center * center + 1e-05)


def stats_kernel(own, r1, r2, r3, conv, sums):
    total = own[...] + r1[...].astype(F32) + r2[...].astype(F32) + r3[...].astype(F32)
    rounded = total.astype(BF)
    conv[...] = rounded
    wide = rounded.astype(F32)
    sums[...] = to_lanes(
        jnp.sum(wide, axis=1, keepdims=True), jnp.sum(wide * wide, axis=1, keepdims=True)
    )


def act_kernel(conv, sums, gain, bias, u0, u1, u2, u3, act, normed, grad_affine, sums2):
    center, inverse = group_stats(sums)
    norm = (conv[...].astype(F32) - center) * inverse
    normed[...] = norm
    affine = norm * column(gain) + column(bias)
    sigmoid = jax.nn.sigmoid(affine)
    act[...] = (affine * sigmoid).astype(BF)
    grad_act = u0[...] + u1[...].astype(F32) + u2[...].astype(F32) + u3[...].astype(F32)
    grad = grad_act * sigmoid * (1.0 + affine * (1.0 - sigmoid))
    grad_affine[...] = grad
    sums2[...] = to_lanes(
        jnp.sum(grad * norm, axis=1, keepdims=True), jnp.sum(grad, axis=1, keepdims=True)
    )


def group_sum(values):
    row = lax.broadcasted_iota(jnp.int32, (BLK, 1), 0)
    low = jnp.sum(jnp.where(row < BLK // 2, values, 0.0), axis=0, keepdims=True)
    high = jnp.sum(jnp.where(row < BLK // 2, 0.0, values), axis=0, keepdims=True)
    return jnp.where(row < BLK // 2, low, high)


def grad_kernel(normed, grad_affine, sums, sums2, gain, grad_conv, totals):
    _, inverse = group_stats(sums)
    row, lane = lane_rows()
    total = jnp.sum(sums2[...], axis=0, keepdims=True)
    totals[...] = total
    scale = column(gain)
    gain_sum = jnp.sum(jnp.where(lane == row, total, 0.0), axis=1, keepdims=True)
    bias_sum = jnp.sum(jnp.where(lane == row + 64, total, 0.0), axis=1, keepdims=True)
    first = group_sum(scale * bias_sum) / MEMBERS
    second = group_sum(scale * gain_sum) / MEMBERS
    value = inverse * (grad_affine[...] * scale - first - normed[...] * second)
    grad_conv[...] = value.astype(BF)


def call(kernel, outs, *args):
    return pl.pallas_call(kernel, out_shape=outs, compiler_params=params(), name=kernel.__name__)(*args)


def body(inputs, spatial_weight, temporal_weight, norm_gain, norm_bias, cotangent):
    x = inputs.reshape(BLK, CELLS)
    cot = cotangent.reshape(BLK, CELLS)
    gain = norm_gain.reshape(1, BLK)
    bias = norm_bias.reshape(1, BLK)

    def flat(spatial, temporal):
        spatial = jnp.pad(spatial.reshape(BLK, 9 * BLK), ((0, 0), (0, SP - 9 * BLK)))
        temporal = jnp.pad(temporal.reshape(BLK, 3 * BLK), ((0, 0), (0, TP - 3 * BLK)))
        return jnp.concatenate([spatial, temporal], 1)

    local = jnp.stack(
        [
            flat(spatial_weight.transpose(1, 0, 2), temporal_weight.transpose(1, 0, 2)),
            flat(spatial_weight.transpose(2, 0, 1), temporal_weight.transpose(2, 0, 1)),
        ]
    )
    xs = [x] + [over_a(x, k) for k in (1, 2, 3)]
    cots = [cot] + [over_b(cot, l) for l in (1, 2, 3)]
    moved = lax.ppermute(local, ("dt", "ch"), piece_moves())
    weights = lax.all_to_all(jnp.broadcast_to(moved, (16,) + moved.shape), "dt", 0, 0)

    cot4 = jnp.stack(cots)
    cot_before, cot_after = neighbours(cot4)
    cot_frames = (cot_after, cot4, cot_before)

    own, s1, s2, s3 = conv_forward(xs, weights)
    received = [over_b(s, l + 1) for l, s in enumerate((s1, s2, s3))]

    u, u1, u2, u3 = time_mix(cot_frames, weights, 0)
    us = [u] + [over_a(s, k + 1) for k, s in enumerate((u1, u2, u3))]

    wide = shape((BLK, CELLS), F32)
    narrow = shape((BLK, CELLS), BF)
    small = shape((16, 128), F32)
    conv, sums = call(stats_kernel, [narrow, small], own, *received)
    sums = lax.all_to_all(sums, "dt", 0, 0, tiled=True)
    act, normed, grad_affine, sums2 = call(
        act_kernel, [narrow, wide, wide, small], conv, sums, gain, bias, *us
    )
    acts = [act] + [over_a(act, k) for k in (1, 2, 3)]
    sums2 = lax.all_to_all(sums2, "dt", 0, 0, tiled=True)
    grad_conv, totals = call(
        grad_kernel, [narrow, shape((1, 128), F32)], normed, grad_affine, sums, sums2, gain
    )
    gs = [grad_conv] + [over_b(grad_conv, l) for l in (1, 2, 3)]

    act4 = jnp.stack(acts)
    temporal_part = time_grad(act4, cot_frames)
    act_before, act_after = neighbours(act4)
    m, m1, m2, m3 = time_mix((act_before, act4, act_after), weights, 1)
    ms = [over_b(s, l + 1) for l, s in enumerate((m1, m2, m3))]
    mixed = m + ms[0].astype(F32) + ms[1].astype(F32) + ms[2].astype(F32)
    output = (x.astype(F32) + mixed).astype(BF)

    d, d1, d2, d3, spatial_part = conv_backward(gs, xs, weights)
    ds = [over_a(s, k + 1) for k, s in enumerate((d1, d2, d3))]
    back = d + ds[0].astype(F32) + ds[1].astype(F32) + ds[2].astype(F32)
    grad_inputs = (cot.astype(F32) + back).astype(BF)

    parts = jnp.concatenate([spatial_part, temporal_part], 2)
    parts = lax.all_to_all(parts, "dt", 0, 0)
    total = jnp.sum(parts, axis=0)
    total = lax.ppermute(total, ("dt", "ch"), [(b, a) for a, b in piece_moves()])
    grad_spatial = total[:, : 9 * BLK].reshape(BLK, 9, BLK).transpose(1, 0, 2)
    grad_temporal = total[:, SP : SP + 3 * BLK].reshape(BLK, 3, BLK).transpose(1, 0, 2)

    return (
        output.reshape(inputs.shape),
        grad_inputs.reshape(inputs.shape),
        grad_spatial,
        grad_temporal,
        totals[0, :BLK],
        totals[0, 64 : 64 + BLK],
    )


def solution(mesh):
    in_specs = (
        P("ch", "dt", None),
        P(None, "ch", "dt"),
        P(None, "ch", "dt"),
        P("ch"),
        P("ch"),
        P("ch", "dt", None),
    )
    out_specs = (
        P("ch", "dt", None),
        P("ch", "dt", None),
        P(None, "ch", "dt"),
        P(None, "ch", "dt"),
        P("ch"),
        P("ch"),
    )
    return jax.shard_map(body, mesh=mesh, in_specs=in_specs, out_specs=out_specs, check_vma=False)
```

```python
import jax
import jax.numpy as jnp
from jax import lax
from jax.experimental import pallas as pl
from jax.experimental.pallas import tpu as pltpu
from jax.sharding import PartitionSpec as P

C = 640
G = 32
W = 64
CELLS = 2304
FRAMES = 16
BLK = 40
MEMBERS = (C // G) * FRAMES * CELLS
TAPS = ((-1, -1), (-1, 0), (-1, 1), (0, -1), (0, 0), (0, 1), (1, -1), (1, 0), (1, 1))
SP = 384
TP = 128
BF = jnp.bfloat16
F32 = jnp.float32

AXES = ("dt", "ch")
CORES = [list(range(0, 16, 2)), list(range(1, 16, 2))]


def split(block):
    return (block >> 1) & 3, ((block >> 3) << 1) | (block & 1)


def join(a, b):
    return ((b >> 1) << 3) | (a << 1) | (b & 1)


def over_a(value, k):
    return lax.ppermute(value, "ch", [(i, i ^ (k << 1)) for i in range(16)])


def over_b(value, l):
    mask = join(0, l)
    return lax.ppermute(value, "ch", [(i, i ^ mask) for i in range(16)])


def piece_moves():
    moves = []
    for into in range(16):
        for out in range(16):
            (a, b), (c, d) = split(into), split(out)
            place = ((a ^ c) * 4 + (b ^ d)) * 16 + join(c, b)
            moves.append((out * 16 + into, place))
    return moves


def neighbours(value):
    before = lax.ppermute(value, "dt", [(i, i + 1) for i in range(15)])
    after = lax.ppermute(value, "dt", [(i + 1, i) for i in range(15)])
    return before, after


def exchange(value):
    return lax.all_to_all(value, "dt", 0, 0)


def exchange8(value):
    return lax.all_to_all(value, "dt", 0, 0, axis_index_groups=CORES)


def other_core(value):
    return lax.ppermute(value, "dt", [(i, i ^ 1) for i in range(16)])


def params(limit=50):
    return pltpu.CompilerParams(vmem_limit_bytes=limit * 1024 * 1024)


def cost(micros=0):
    return pl.CostEstimate(flops=0, bytes_accessed=max(1, micros * 3000000), transcendentals=0)


def shape(dims, dtype):
    return jax.ShapeDtypeStruct(dims, dtype)


def shifted(value, row_step, col_step):
    cell = lax.broadcasted_iota(jnp.int32, (1, CELLS), 1)
    col = cell & (W - 1)
    inside = jnp.ones((1, CELLS), F32)
    if row_step == -1:
        inside = jnp.where(cell >= W, inside, 0.0)
    if row_step == 1:
        inside = jnp.where(cell < CELLS - W, inside, 0.0)
    if col_step == -1:
        inside = jnp.where(col >= 1, inside, 0.0)
    if col_step == 1:
        inside = jnp.where(col < W - 1, inside, 0.0)
    step = row_step * W + col_step
    if step == 0:
        return value
    return pltpu.roll(value, (-step) % CELLS, 1) * inside


def fill_taps(taps_ref, base, value, direction):
    wide = value.astype(F32)
    held = []
    for t, (a, b) in enumerate(TAPS):
        held.append(shifted(wide, direction * a, direction * b))
        if len(held) == 2:
            taps_ref[pl.ds(base + (t - 1) * BLK, 2 * BLK), :] = jnp.concatenate(held, 0).astype(BF)
            held = []
    held.append(jnp.zeros((SP - 9 * BLK, CELLS), F32))
    taps_ref[pl.ds(base + 8 * BLK, SP - 8 * BLK), :] = jnp.concatenate(held, 0).astype(BF)


class Pieces:
    def __init__(self, core, own, other):
        self.keep = 1.0 - core[0].astype(F32)
        self.refs = own, other

    def get(self, k, l, first, width):
        n = k * 4 + l
        own, other = [ref[n >> 1, :, first : first + width].astype(F32) for ref in self.refs]
        if n & 1:
            own, other = other, own
        return own * self.keep + other * (1.0 - self.keep)


def left_matrix(pieces, flipped, first, width):
    rows = []
    for r in range(4):
        parts = []
        for c in range(4):
            if flipped:
                turned = pieces.get(c, r, first, width).T
                count = width // BLK
                blocks = [turned[t * BLK : (t + 1) * BLK] for t in range(count)]
                blocks.append(jnp.zeros((BLK, width - count * BLK), F32))
                parts.append(jnp.concatenate(blocks, 1))
            else:
                parts.append(pieces.get(r, c, first, width))
        rows.append(jnp.concatenate(parts, 1))
    return jnp.concatenate(rows, 0).astype(BF)


def spread(left, right_ref, own_ref, send_refs):
    width = 256

    def chunk(c, carry):
        cols = pl.ds(pl.multiple_of(c * width, width), width)
        part = jnp.dot(left, right_ref[:, cols], preferred_element_type=F32)
        own_ref[:, cols] = part[:BLK]
        for n, ref in enumerate(send_refs):
            ref[:, cols] = part[(n + 1) * BLK : (n + 2) * BLK].astype(BF)
        return carry

    lax.fori_loop(0, CELLS // width, chunk, 0)


PARTIALS = [shape((BLK, CELLS), F32)] + [shape((BLK, CELLS), BF)] * 3


VMEM = pl.BlockSpec(memory_space=pltpu.VMEM)
SMEM = pl.BlockSpec(memory_space=pltpu.SMEM)
HBM = pl.BlockSpec(memory_space=pl.ANY)


def conv_kernel(core, w_own, w_other, x0, x1, x2, x3, own, s1, s2, s3, taps):
    for k, ref in enumerate((x0, x1, x2, x3)):
        fill_taps(taps, k * SP, ref[...], 1)
    left = left_matrix(Pieces(core, w_own, w_other), True, 0, SP)
    spread(left, taps, own, (s1, s2, s3))


def conv_forward(xs, weights):
    return pl.pallas_call(
        conv_kernel,
        out_shape=PARTIALS,
        in_specs=[SMEM] + [VMEM] * 6,
        scratch_shapes=[pltpu.VMEM((4 * SP, CELLS), BF)],
        compiler_params=params(),
        cost_estimate=cost(),
        name="conv_forward",
    )(*weights, *xs)


def back_kernel(*refs):
    core, w_own, w_other = refs[:3]
    gs, xs = refs[3:7], refs[7:11]
    own, s1, s2, s3, grad, grad_other, taps = refs[-7:]
    for l in range(4):
        fill_taps(taps, l * SP, gs[l][...], -1)
    left = left_matrix(Pieces(core, w_own, w_other), False, 0, SP)
    spread(left, taps, own, (s1, s2, s3))
    field = jnp.concatenate([ref[...].astype(F32) for ref in xs], 0).astype(BF)
    products = [
        lax.dot_general(
            field, taps[l * SP : (l + 1) * SP, :], (((1,), (1,)), ((), ())), preferred_element_type=F32
        )
        for l in range(4)
    ]
    put_pieces(core, products, grad, grad_other, 0, SP)


def put_pieces(core, products, own, other, first, width):
    keep = 1.0 - core[0].astype(F32)
    for k in range(4):
        for l in (0, 2):
            even = products[l][k * BLK : (k + 1) * BLK]
            odd = products[l + 1][k * BLK : (k + 1) * BLK]
            n = (k * 4 + l) >> 1
            own[n, :, first : first + width] = even * keep + odd * (1.0 - keep)
            other[n, :, first : first + width] = even * (1.0 - keep) + odd * keep


def conv_backward(gs, xs, weights, after):
    return pl.pallas_call(
        back_kernel,
        out_shape=PARTIALS + [shape((8, BLK, SP), F32)] * 2,
        in_specs=[SMEM] + [VMEM] * 10 + [HBM] * len(after),
        out_specs=[VMEM] * 6,
        scratch_shapes=[pltpu.VMEM((4 * SP, CELLS), BF)],
        compiler_params=params(),
        cost_estimate=cost(),
        name="conv_backward",
    )(*weights, *gs, *xs, *after)


def fill_frames(stack_ref, frames):
    for n in range(4):
        parts = [ref[n].astype(F32) for ref in frames]
        parts.append(jnp.zeros((TP - 3 * BLK, CELLS), F32))
        stack_ref[n * TP : (n + 1) * TP, :] = jnp.concatenate(parts, 0).astype(BF)


def time_mix(frames, weights, flipped):
    def kernel(core, w_own, w_other, first, second, third, own, s1, s2, s3, stack):
        fill_frames(stack, (first, second, third))
        left = left_matrix(Pieces(core, w_own, w_other), flipped, SP, TP)
        spread(left, stack, own, (s1, s2, s3))

    return pl.pallas_call(
        kernel,
        out_shape=PARTIALS,
        in_specs=[SMEM] + [VMEM] * 5,
        scratch_shapes=[pltpu.VMEM((4 * TP, CELLS), BF)],
        compiler_params=params(),
        cost_estimate=cost(),
        name="time_mix",
    )(*weights, *frames)


def time_grad_kernel(core, act, first, second, third, grad, grad_other, stack):
    fill_frames(stack, (first, second, third))
    field = jnp.concatenate([act[k].astype(F32) for k in range(4)], 0).astype(BF)
    part = lax.dot_general(field, stack[...], (((1,), (1,)), ((), ())), preferred_element_type=F32)
    products = [part[:, l * TP : (l + 1) * TP] for l in range(4)]
    put_pieces(core, products, grad, grad_other, 0, TP)


def time_grad(core, act4, frames):
    return pl.pallas_call(
        time_grad_kernel,
        out_shape=[shape((8, BLK, TP), F32)] * 2,
        in_specs=[SMEM] + [VMEM] * 4,
        scratch_shapes=[pltpu.VMEM((4 * TP, CELLS), BF)],
        compiler_params=params(),
        cost_estimate=cost(),
        name="time_grad",
    )(core, act4, *frames)


def hold_kernel(value, *refs):
    refs[-1][...] = value[...]


def hold_after(value, after):
    return pl.pallas_call(
        hold_kernel,
        out_shape=shape(value.shape, value.dtype),
        in_specs=[VMEM] + [HBM] * len(after),
        compiler_params=params(),
        cost_estimate=cost(),
        name="hold_after",
    )(value, *after)


def stack_kernel(p0, p1, p2, p3, *refs):
    for n, ref in enumerate((p0, p1, p2, p3)):
        refs[-1][n] = ref[...]


def stack_after(parts, after):
    return pl.pallas_call(
        stack_kernel,
        out_shape=shape((4, BLK, CELLS), BF),
        in_specs=[VMEM] * 4 + [HBM] * len(after),
        compiler_params=params(),
        cost_estimate=cost(),
        name="stack_after",
    )(*parts, *after)


def merge_kernel(spatial, temporal, out):
    out[:, :, 0:SP] = spatial[...]
    out[:, :, SP:] = temporal[...]


def pair_kernel(s0, t0, received, *refs):
    out = refs[-1]
    out[:, :, 0:SP] = s0[...] + received[:, :, 0:SP]
    out[:, :, SP:] = t0[...] + received[:, :, SP:]


def pair_sum(s0, t0, received, after):
    return pl.pallas_call(
        pair_kernel,
        out_shape=shape((8, BLK, SP + TP), F32),
        in_specs=[VMEM] * 3 + [HBM] * len(after),
        compiler_params=params(),
        cost_estimate=cost(),
        name="pair_sum",
    )(s0, t0, received, *after)


def prepare_kernel(spatial, temporal, out):
    def row(pieces, width):
        filler = jnp.zeros((BLK, width - len(pieces) * BLK), F32)
        return jnp.concatenate(pieces + [filler], 1)

    first = [spatial[t].astype(F32) for t in range(9)]
    second = [temporal[t].astype(F32) for t in range(3)]
    out[...] = jnp.concatenate([row(first, SP), row(second, TP)], 1).astype(BF)


def add_up(own, r1, r2, r3):
    return own[...] + r1[...].astype(F32) + r2[...].astype(F32) + r3[...].astype(F32)


def lane_rows():
    return (
        lax.broadcasted_iota(jnp.int32, (BLK, 128), 0),
        lax.broadcasted_iota(jnp.int32, (BLK, 128), 1),
    )


def to_lanes(low, high):
    row, lane = lane_rows()
    both = jnp.where(lane == row, low, 0.0) + jnp.where(lane == row + 64, high, 0.0)
    return jnp.sum(both, axis=0, keepdims=True)


def column(row_ref):
    row = lax.broadcasted_iota(jnp.int32, (BLK, BLK), 0)
    lane = lax.broadcasted_iota(jnp.int32, (BLK, BLK), 1)
    return jnp.sum(jnp.where(row == lane, row_ref[...], 0.0), axis=1, keepdims=True)


def group_sum(values):
    row = lax.broadcasted_iota(jnp.int32, (BLK, 1), 0)
    low = jnp.sum(jnp.where(row < BLK // 2, values, 0.0), axis=0, keepdims=True)
    high = jnp.sum(jnp.where(row < BLK // 2, 0.0, values), axis=0, keepdims=True)
    return jnp.where(row < BLK // 2, low, high)


def put_sums(sums, low, high):
    sums[...] = jnp.broadcast_to(to_lanes(low, high).reshape(1, 1, 128), (16, 1, 128))


def get_sums(sums):
    total = jnp.sum(sums[...], axis=0)
    row, lane = lane_rows()
    low = jnp.sum(jnp.where(lane == row, total, 0.0), axis=1, keepdims=True)
    high = jnp.sum(jnp.where(lane == row + 64, total, 0.0), axis=1, keepdims=True)
    return total, low, high


def stats_kernel(own, r1, r2, r3, conv, sums):
    rounded = add_up(own, r1, r2, r3).astype(BF)
    conv[...] = rounded
    wide = rounded.astype(F32)
    put_sums(
        sums, jnp.sum(wide, axis=1, keepdims=True), jnp.sum(wide * wide, axis=1, keepdims=True)
    )


def act_kernel(conv, sums, gain, bias, u0, u1, u2, u3, act, normed, grad_affine, inv, sums2):
    _, low, high = get_sums(sums)
    center = group_sum(low) / MEMBERS
    inverse = lax.rsqrt(group_sum(high) / MEMBERS - center * center + 1e-05)
    inv[...] = jnp.broadcast_to(inverse, (BLK, 128))
    norm = (conv[...].astype(F32) - center) * inverse
    normed[...] = norm
    affine = norm * column(gain) + column(bias)
    sigmoid = jax.nn.sigmoid(affine)
    act[...] = (affine * sigmoid).astype(BF)
    grad = add_up(u0, u1, u2, u3) * sigmoid * (1.0 + affine * (1.0 - sigmoid))
    grad_affine[...] = grad
    put_sums(
        sums2, jnp.sum(grad * norm, axis=1, keepdims=True), jnp.sum(grad, axis=1, keepdims=True)
    )


def grad_kernel(normed, grad_affine, inv, sums2, gain, grad_conv, totals):
    total, gain_sum, bias_sum = get_sums(sums2)
    totals[...] = total
    scale = column(gain)
    first = group_sum(scale * bias_sum) / MEMBERS
    second = group_sum(scale * gain_sum) / MEMBERS
    value = inv[:, 0:1] * (grad_affine[...] * scale - first - normed[...] * second)
    grad_conv[...] = value.astype(BF)


def finish_kernel(start, own, r1, r2, r3, out):
    out[...] = (start[...].astype(F32) + add_up(own, r1, r2, r3)).astype(BF)


def total_kernel(parts, total):
    total[...] = jnp.sum(parts[...], axis=0)


def final_kernel(total, spatial, temporal):
    value = total[...]
    for t in range(9):
        spatial[t] = value[:, t * BLK : (t + 1) * BLK]
    for t in range(3):
        temporal[t] = value[:, SP + t * BLK : SP + (t + 1) * BLK]


def repeat_kernel(value, *refs):
    out = refs[-1]
    for n in range(8):
        out[n] = value[...]


def repeat_after(value, *after):
    vmem = pl.BlockSpec(memory_space=pltpu.VMEM)
    return pl.pallas_call(
        repeat_kernel,
        out_shape=shape((8,) + value.shape, value.dtype),
        in_specs=[vmem] + [pl.BlockSpec(memory_space=pl.ANY)] * len(after),
        out_specs=vmem,
        compiler_params=params(),
        cost_estimate=cost(),
        name="repeat_after",
    )(value, *after)


def call(kernel, outs, *args, limit=50, micros=0):
    return pl.pallas_call(
        kernel,
        out_shape=outs,
        compiler_params=params(limit),
        cost_estimate=cost(micros),
        name=kernel.__name__,
    )(*args)


def body(inputs, spatial_weight, temporal_weight, norm_gain, norm_bias, cotangent):
    wide = shape((BLK, CELLS), F32)
    narrow = shape((BLK, CELLS), BF)
    small = shape((16, 1, 128), F32)
    core = (lax.axis_index("dt") & 1).reshape(1)
    x, cot = inputs.reshape(BLK, CELLS), cotangent.reshape(BLK, CELLS)
    gain, bias = norm_gain.reshape(1, BLK), norm_bias.reshape(1, BLK)

    local = call(prepare_kernel, shape((BLK, SP + TP), BF), spatial_weight, temporal_weight)
    xs = [x] + [over_a(x, k) for k in (1, 2, 3)]
    cots = [cot] + [over_b(cot, l) for l in (1, 2, 3)]
    moved = lax.ppermute(local, AXES, piece_moves())
    w_own = exchange8(repeat_after(moved, *xs[1:], *cots[1:]))
    weights = core, w_own, other_core(w_own)

    cot4 = stack_after(cots, (moved,))
    cot_before, cot_after = neighbours(cot4)
    cot_frames = (cot_after, cot4, cot_before)

    own, s1, s2, s3 = conv_forward(xs, weights)
    received = [over_b(s, l + 1) for l, s in enumerate((s1, s2, s3))]
    u, u1, u2, u3 = time_mix(cot_frames, weights, False)
    us = [u] + [over_a(s, k + 1) for k, s in enumerate((u1, u2, u3))]

    conv, sums = call(stats_kernel, [narrow, small], own, *received)
    act, normed, grad_affine, inv, sums2 = call(
        act_kernel,
        [narrow, wide, wide, shape((BLK, 128), F32), small],
        conv, exchange(sums), gain, bias, *us,
    )
    acts = [act] + [over_a(act, k) for k in (1, 2, 3)]
    grad_conv, totals = call(
        grad_kernel,
        [narrow, shape((1, 128), F32)],
        normed, grad_affine, inv, exchange(sums2), gain,
    )
    gs = [grad_conv] + [over_b(grad_conv, l) for l in (1, 2, 3)]
    act4 = stack_after(acts, (grad_conv,))
    before, after = neighbours(hold_after(act4, gs[1:]))

    d, d1, d2, d3, s_own, s_other = conv_backward(gs, xs, weights, ())
    ds = [over_a(s, k + 1) for k, s in enumerate((d1, d2, d3))]
    t_own, t_other = time_grad(core, act4, cot_frames)
    m, m1, m2, m3 = time_mix((before, act4, after), weights, True)
    ms = [over_b(s, l + 1) for l, s in enumerate((m1, m2, m3))]

    received = other_core(call(merge_kernel, shape((8, BLK, SP + TP), F32), s_other, t_other))
    parts = exchange8(pair_sum(s_own, t_own, received, ()))
    total = call(total_kernel, shape((BLK, SP + TP), F32), parts)
    total = lax.ppermute(total, AXES, [(b, a) for a, b in piece_moves()])
    grad_spatial, grad_temporal = call(
        final_kernel, [shape((9, BLK, BLK), F32), shape((3, BLK, BLK), F32)], total
    )
    grad_inputs = call(finish_kernel, narrow, cot, d, *ds)
    output = call(finish_kernel, narrow, x, m, *ms)

    return (
        output.reshape(inputs.shape),
        grad_inputs.reshape(inputs.shape),
        grad_spatial,
        grad_temporal,
        totals[0, :BLK],
        totals[0, 64 : 64 + BLK],
    )


def solution(mesh):
    in_specs = (
        P("ch", "dt", None),
        P(None, "ch", "dt"),
        P(None, "ch", "dt"),
        P("ch"),
        P("ch"),
        P("ch", "dt", None),
    )
    out_specs = (
        P("ch", "dt", None),
        P("ch", "dt", None),
        P(None, "ch", "dt"),
        P(None, "ch", "dt"),
        P("ch"),
        P("ch"),
    )
    return jax.shard_map(body, mesh=mesh, in_specs=in_specs, out_specs=out_specs, check_vma=False)
```

```python
import jax
import jax.numpy as jnp
from jax import lax
from jax.experimental import pallas as pl
from jax.experimental.pallas import tpu as pltpu
from jax.sharding import PartitionSpec as P

C = 640
G = 32
W = 64
CELLS = 2304
FRAMES = 16
BLK = 40
MEMBERS = (C // G) * FRAMES * CELLS
TAPS = ((-1, -1), (-1, 0), (-1, 1), (0, -1), (0, 0), (0, 1), (1, -1), (1, 0), (1, 1))
SP = 384
TP = 128
BF = jnp.bfloat16
F32 = jnp.float32

AXES = ("dt", "ch")
CORES = [list(range(0, 16, 2)), list(range(1, 16, 2))]


def split(block):
    return (block >> 1) & 3, ((block >> 3) << 1) | (block & 1)


def join(a, b):
    return ((b >> 1) << 3) | (a << 1) | (b & 1)


def over_a(value, k):
    return lax.ppermute(value, "ch", [(i, i ^ (k << 1)) for i in range(16)])


def over_b(value, l):
    mask = join(0, l)
    return lax.ppermute(value, "ch", [(i, i ^ mask) for i in range(16)])


def piece_moves():
    moves = []
    for into in range(16):
        for out in range(16):
            (a, b), (c, d) = split(into), split(out)
            place = ((a ^ c) * 4 + (b ^ d)) * 16 + join(c, b)
            moves.append((out * 16 + into, place))
    return moves


def neighbours(value):
    before = lax.ppermute(value, "dt", [(i, i + 1) for i in range(15)])
    after = lax.ppermute(value, "dt", [(i + 1, i) for i in range(15)])
    return before, after


def exchange(value):
    return lax.all_to_all(value, "dt", 0, 0)


def exchange8(value):
    return lax.all_to_all(value, "dt", 0, 0, axis_index_groups=CORES)


def other_core(value):
    return lax.ppermute(value, "dt", [(i, i ^ 1) for i in range(16)])


def params(limit=50):
    return pltpu.CompilerParams(vmem_limit_bytes=limit * 1024 * 1024)


def cost(micros=0):
    return pl.CostEstimate(flops=0, bytes_accessed=max(1, micros * 3000000), transcendentals=0)


def shape(dims, dtype):
    return jax.ShapeDtypeStruct(dims, dtype)


def shifted(value, row_step, col_step):
    cell = lax.broadcasted_iota(jnp.int32, (1, CELLS), 1)
    col = cell & (W - 1)
    inside = jnp.ones((1, CELLS), F32)
    if row_step == -1:
        inside = jnp.where(cell >= W, inside, 0.0)
    if row_step == 1:
        inside = jnp.where(cell < CELLS - W, inside, 0.0)
    if col_step == -1:
        inside = jnp.where(col >= 1, inside, 0.0)
    if col_step == 1:
        inside = jnp.where(col < W - 1, inside, 0.0)
    step = row_step * W + col_step
    if step == 0:
        return value
    return pltpu.roll(value, (-step) % CELLS, 1) * inside


def fill_taps(taps_ref, base, value, direction):
    wide = value.astype(F32)
    held = []
    for t, (a, b) in enumerate(TAPS):
        held.append(shifted(wide, direction * a, direction * b))
        if len(held) == 2:
            taps_ref[pl.ds(base + (t - 1) * BLK, 2 * BLK), :] = jnp.concatenate(held, 0).astype(BF)
            held = []
    held.append(jnp.zeros((SP - 9 * BLK, CELLS), F32))
    taps_ref[pl.ds(base + 8 * BLK, SP - 8 * BLK), :] = jnp.concatenate(held, 0).astype(BF)


class Pieces:
    def __init__(self, core, own, other):
        self.keep = 1.0 - core[0].astype(F32)
        self.refs = own, other

    def get(self, k, l, first, width):
        n = k * 4 + l
        own, other = [ref[n >> 1, :, first : first + width].astype(F32) for ref in self.refs]
        if n & 1:
            own, other = other, own
        return own * self.keep + other * (1.0 - self.keep)


def left_matrix(pieces, flipped, first, width):
    rows = []
    for r in range(4):
        parts = []
        for c in range(4):
            if flipped:
                turned = pieces.get(c, r, first, width).T
                count = width // BLK
                blocks = [turned[t * BLK : (t + 1) * BLK] for t in range(count)]
                blocks.append(jnp.zeros((BLK, width - count * BLK), F32))
                parts.append(jnp.concatenate(blocks, 1))
            else:
                parts.append(pieces.get(r, c, first, width))
        rows.append(jnp.concatenate(parts, 1))
    return jnp.concatenate(rows, 0).astype(BF)


def spread(left, right_ref, own_ref, send_refs):
    width = 256

    def chunk(c, carry):
        cols = pl.ds(pl.multiple_of(c * width, width), width)
        part = jnp.dot(left, right_ref[:, cols], preferred_element_type=F32)
        own_ref[:, cols] = part[:BLK]
        for n, ref in enumerate(send_refs):
            ref[:, cols] = part[(n + 1) * BLK : (n + 2) * BLK].astype(BF)
        return carry

    lax.fori_loop(0, CELLS // width, chunk, 0)


PARTIALS = [shape((BLK, CELLS), F32)] + [shape((BLK, CELLS), BF)] * 3


VMEM = pl.BlockSpec(memory_space=pltpu.VMEM)
SMEM = pl.BlockSpec(memory_space=pltpu.SMEM)
HBM = pl.BlockSpec(memory_space=pl.ANY)


def left_kernel(core, w_own, w_other, first, second, third, fourth):
    pieces = Pieces(core, w_own, w_other)
    first[...] = left_matrix(pieces, True, 0, SP)
    second[...] = left_matrix(pieces, False, 0, SP)
    third[...] = left_matrix(pieces, False, SP, TP)
    fourth[...] = left_matrix(pieces, True, SP, TP)


def left_matrices(core, w_own, w_other):
    return pl.pallas_call(
        left_kernel,
        out_shape=[shape((4 * BLK, 4 * width), BF) for width in (SP, SP, TP, TP)],
        in_specs=[SMEM] + [VMEM] * 2,
        compiler_params=params(),
        cost_estimate=cost(),
        name="left_matrices",
    )(core, w_own, w_other)


def conv_kernel(left, x0, x1, x2, x3, own, s1, s2, s3, taps):
    for k, ref in enumerate((x0, x1, x2, x3)):
        fill_taps(taps, k * SP, ref[...], 1)
    spread(left[...], taps, own, (s1, s2, s3))


def conv_forward(xs, left):
    return pl.pallas_call(
        conv_kernel,
        out_shape=PARTIALS,
        in_specs=[VMEM] * 5,
        scratch_shapes=[pltpu.VMEM((4 * SP, CELLS), BF)],
        compiler_params=params(),
        cost_estimate=cost(),
        name="conv_forward",
    )(left, *xs)


def back_kernel(*refs):
    core, left = refs[:2]
    gs, xs = refs[2:6], refs[6:10]
    own, s1, s2, s3, grad, grad_other, taps = refs[-7:]
    for l in range(4):
        fill_taps(taps, l * SP, gs[l][...], -1)
    spread(left[...], taps, own, (s1, s2, s3))
    field = jnp.concatenate([ref[...].astype(F32) for ref in xs], 0).astype(BF)
    products = [
        lax.dot_general(
            field, taps[l * SP : (l + 1) * SP, :], (((1,), (1,)), ((), ())), preferred_element_type=F32
        )
        for l in range(4)
    ]
    put_pieces(core, products, grad, grad_other, 0, SP)


def put_pieces(core, products, own, other, first, width):
    keep = 1.0 - core[0].astype(F32)
    for k in range(4):
        for l in (0, 2):
            even = products[l][k * BLK : (k + 1) * BLK]
            odd = products[l + 1][k * BLK : (k + 1) * BLK]
            n = (k * 4 + l) >> 1
            own[n, :, first : first + width] = even * keep + odd * (1.0 - keep)
            other[n, :, first : first + width] = even * (1.0 - keep) + odd * keep


def conv_backward(core, left, gs, xs):
    return pl.pallas_call(
        back_kernel,
        out_shape=PARTIALS + [shape((8, BLK, SP), F32)] * 2,
        in_specs=[SMEM] + [VMEM] * 9,
        out_specs=[VMEM] * 6,
        scratch_shapes=[pltpu.VMEM((4 * SP, CELLS), BF)],
        compiler_params=params(),
        cost_estimate=cost(),
        name="conv_backward",
    )(core, left, *gs, *xs)


def fill_frames(stack_ref, frames):
    for n in range(4):
        parts = [ref[n].astype(F32) for ref in frames]
        parts.append(jnp.zeros((TP - 3 * BLK, CELLS), F32))
        stack_ref[n * TP : (n + 1) * TP, :] = jnp.concatenate(parts, 0).astype(BF)


def time_mix_kernel(left, first, second, third, own, s1, s2, s3, stack):
    fill_frames(stack, (first, second, third))
    spread(left[...], stack, own, (s1, s2, s3))


def time_mix(left, frames):
    return pl.pallas_call(
        time_mix_kernel,
        out_shape=PARTIALS,
        in_specs=[VMEM] * 4,
        scratch_shapes=[pltpu.VMEM((4 * TP, CELLS), BF)],
        compiler_params=params(),
        cost_estimate=cost(),
        name="time_mix",
    )(left, *frames)


def time_grad_kernel(core, act, first, second, third, grad, grad_other, stack):
    fill_frames(stack, (first, second, third))
    field = jnp.concatenate([act[k].astype(F32) for k in range(4)], 0).astype(BF)
    part = lax.dot_general(field, stack[...], (((1,), (1,)), ((), ())), preferred_element_type=F32)
    products = [part[:, l * TP : (l + 1) * TP] for l in range(4)]
    put_pieces(core, products, grad, grad_other, 0, TP)


def time_grad(core, act4, frames):
    return pl.pallas_call(
        time_grad_kernel,
        out_shape=[shape((8, BLK, TP), F32)] * 2,
        in_specs=[SMEM] + [VMEM] * 4,
        scratch_shapes=[pltpu.VMEM((4 * TP, CELLS), BF)],
        compiler_params=params(),
        cost_estimate=cost(),
        name="time_grad",
    )(core, act4, *frames)


def hold_kernel(value, *refs):
    refs[-1][...] = value[...]


def hold_after(value, after):
    return pl.pallas_call(
        hold_kernel,
        out_shape=shape(value.shape, value.dtype),
        in_specs=[VMEM] + [HBM] * len(after),
        compiler_params=params(),
        cost_estimate=cost(),
        name="hold_after",
    )(value, *after)


def stack_kernel(p0, p1, p2, p3, *refs):
    for n, ref in enumerate((p0, p1, p2, p3)):
        refs[-1][n] = ref[...]


def stack_after(parts, after):
    return pl.pallas_call(
        stack_kernel,
        out_shape=shape((4, BLK, CELLS), BF),
        in_specs=[VMEM] * 4 + [HBM] * len(after),
        compiler_params=params(),
        cost_estimate=cost(),
        name="stack_after",
    )(*parts, *after)


def merge_kernel(spatial, temporal, out):
    out[:, :, 0:SP] = spatial[...]
    out[:, :, SP:] = temporal[...]


def pair_kernel(s0, t0, received, *refs):
    out = refs[-1]
    out[:, :, 0:SP] = (s0[...] + received[:, :, 0:SP]).astype(BF)
    out[:, :, SP:] = (t0[...] + received[:, :, SP:]).astype(BF)


def pair_sum(s0, t0, received, after):
    return pl.pallas_call(
        pair_kernel,
        out_shape=shape((8, BLK, SP + TP), BF),
        in_specs=[VMEM] * 3 + [HBM] * len(after),
        compiler_params=params(),
        cost_estimate=cost(),
        name="pair_sum",
    )(s0, t0, received, *after)


def prepare_kernel(spatial, temporal, out):
    def row(pieces, width):
        filler = jnp.zeros((BLK, width - len(pieces) * BLK), F32)
        return jnp.concatenate(pieces + [filler], 1)

    first = [spatial[t].astype(F32) for t in range(9)]
    second = [temporal[t].astype(F32) for t in range(3)]
    out[...] = jnp.concatenate([row(first, SP), row(second, TP)], 1).astype(BF)


def add_up(own, r1, r2, r3):
    return own[...] + r1[...].astype(F32) + r2[...].astype(F32) + r3[...].astype(F32)


def lane_rows():
    return (
        lax.broadcasted_iota(jnp.int32, (BLK, 128), 0),
        lax.broadcasted_iota(jnp.int32, (BLK, 128), 1),
    )


def to_lanes(low, high):
    row, lane = lane_rows()
    both = jnp.where(lane == row, low, 0.0) + jnp.where(lane == row + 64, high, 0.0)
    return jnp.sum(both, axis=0, keepdims=True)


def column(row_ref):
    row = lax.broadcasted_iota(jnp.int32, (BLK, BLK), 0)
    lane = lax.broadcasted_iota(jnp.int32, (BLK, BLK), 1)
    return jnp.sum(jnp.where(row == lane, row_ref[...], 0.0), axis=1, keepdims=True)


def group_sum(values):
    row = lax.broadcasted_iota(jnp.int32, (BLK, 1), 0)
    low = jnp.sum(jnp.where(row < BLK // 2, values, 0.0), axis=0, keepdims=True)
    high = jnp.sum(jnp.where(row < BLK // 2, 0.0, values), axis=0, keepdims=True)
    return jnp.where(row < BLK // 2, low, high)


def put_sums(sums, low, high):
    sums[...] = jnp.broadcast_to(to_lanes(low, high).reshape(1, 1, 128), (16, 1, 128))


def get_sums(sums):
    total = jnp.sum(sums[...], axis=0)
    row, lane = lane_rows()
    low = jnp.sum(jnp.where(lane == row, total, 0.0), axis=1, keepdims=True)
    high = jnp.sum(jnp.where(lane == row + 64, total, 0.0), axis=1, keepdims=True)
    return total, low, high


def stats_kernel(own, r1, r2, r3, conv, sums):
    rounded = add_up(own, r1, r2, r3).astype(BF)
    conv[...] = rounded
    wide = rounded.astype(F32)
    put_sums(
        sums, jnp.sum(wide, axis=1, keepdims=True), jnp.sum(wide * wide, axis=1, keepdims=True)
    )


def act_kernel(conv, sums, gain, bias, u0, u1, u2, u3, act, normed, grad_affine, inv, sums2):
    _, low, high = get_sums(sums)
    center = group_sum(low) / MEMBERS
    inverse = lax.rsqrt(group_sum(high) / MEMBERS - center * center + 1e-05)
    inv[...] = jnp.broadcast_to(inverse, (BLK, 128))
    norm = (conv[...].astype(F32) - center) * inverse
    normed[...] = norm
    affine = norm * column(gain) + column(bias)
    sigmoid = jax.nn.sigmoid(affine)
    act[...] = (affine * sigmoid).astype(BF)
    grad = add_up(u0, u1, u2, u3) * sigmoid * (1.0 + affine * (1.0 - sigmoid))
    grad_affine[...] = grad
    put_sums(
        sums2, jnp.sum(grad * norm, axis=1, keepdims=True), jnp.sum(grad, axis=1, keepdims=True)
    )


def grad_kernel(normed, grad_affine, inv, sums2, gain, grad_conv, totals):
    total, gain_sum, bias_sum = get_sums(sums2)
    totals[...] = total
    scale = column(gain)
    first = group_sum(scale * bias_sum) / MEMBERS
    second = group_sum(scale * gain_sum) / MEMBERS
    value = inv[:, 0:1] * (grad_affine[...] * scale - first - normed[...] * second)
    grad_conv[...] = value.astype(BF)


def finish_kernel(start, own, r1, r2, r3, *refs):
    refs[-1][...] = (start[...].astype(F32) + add_up(own, r1, r2, r3)).astype(BF)


def finish_after(values, after):
    return pl.pallas_call(
        finish_kernel,
        out_shape=shape((BLK, CELLS), BF),
        in_specs=[VMEM] * 5 + [HBM] * len(after),
        compiler_params=params(),
        cost_estimate=cost(),
        name="finish_after",
    )(*values, *after)


def total_kernel(parts, total):
    total[...] = jnp.sum(parts[...].astype(F32), axis=0)


def final_kernel(total, spatial, temporal):
    value = total[...]
    for t in range(9):
        spatial[t] = value[:, t * BLK : (t + 1) * BLK]
    for t in range(3):
        temporal[t] = value[:, SP + t * BLK : SP + (t + 1) * BLK]


def repeat_kernel(value, *refs):
    out = refs[-1]
    for n in range(8):
        out[n] = value[...]


def repeat_after(value, *after):
    vmem = pl.BlockSpec(memory_space=pltpu.VMEM)
    return pl.pallas_call(
        repeat_kernel,
        out_shape=shape((8,) + value.shape, value.dtype),
        in_specs=[vmem] + [pl.BlockSpec(memory_space=pl.ANY)] * len(after),
        out_specs=vmem,
        compiler_params=params(),
        cost_estimate=cost(),
        name="repeat_after",
    )(value, *after)


def call(kernel, outs, *args, limit=50, micros=0):
    return pl.pallas_call(
        kernel,
        out_shape=outs,
        compiler_params=params(limit),
        cost_estimate=cost(micros),
        name=kernel.__name__,
    )(*args)


def body(inputs, spatial_weight, temporal_weight, norm_gain, norm_bias, cotangent):
    wide = shape((BLK, CELLS), F32)
    narrow = shape((BLK, CELLS), BF)
    small = shape((16, 1, 128), F32)
    core = (lax.axis_index("dt") & 1).reshape(1)
    x, cot = inputs.reshape(BLK, CELLS), cotangent.reshape(BLK, CELLS)
    gain, bias = norm_gain.reshape(1, BLK), norm_bias.reshape(1, BLK)

    local = call(prepare_kernel, shape((BLK, SP + TP), BF), spatial_weight, temporal_weight)
    moved = lax.ppermute(local, AXES, piece_moves())
    xs = [x] + [over_a(x, k) for k in (1, 2, 3)]
    cots = [cot] + [over_b(cot, l) for l in (1, 2, 3)]
    w_own = exchange8(repeat_after(moved, xs[2], cots[3]))
    lefts = left_matrices(core, w_own, other_core(w_own))

    cot4 = stack_after(cots, (moved,))
    cot_before, cot_after = neighbours(cot4)
    cot_frames = (cot_after, cot4, cot_before)

    own, s1, s2, s3 = conv_forward(xs, lefts[0])
    received = [over_b(s, l + 1) for l, s in enumerate((s1, s2, s3))]
    u, u1, u2, u3 = time_mix(lefts[2], cot_frames)
    us = [u] + [over_a(s, k + 1) for k, s in enumerate((u1, u2, u3))]

    conv, sums = call(stats_kernel, [narrow, small], own, *received)
    act, normed, grad_affine, inv, sums2 = call(
        act_kernel,
        [narrow, wide, wide, shape((BLK, 128), F32), small],
        conv, exchange(sums), gain, bias, *us,
    )
    acts = [act] + [over_a(act, k) for k in (1, 2, 3)]
    grad_conv, totals = call(
        grad_kernel,
        [narrow, shape((1, 128), F32)],
        normed, grad_affine, inv, exchange(sums2), gain,
    )
    gs = [grad_conv] + [over_b(grad_conv, l) for l in (1, 2, 3)]
    act4 = stack_after(acts, (grad_conv,))
    before, after = neighbours(hold_after(act4, gs[1:]))

    d, d1, d2, d3, s_own, s_other = conv_backward(core, lefts[1], gs, xs)
    ds = [over_a(s, k + 1) for k, s in enumerate((d1, d2, d3))]
    t_own, t_other = time_grad(core, act4, cot_frames)

    received = other_core(call(merge_kernel, shape((8, BLK, SP + TP), F32), s_other, t_other))
    parts = exchange8(pair_sum(s_own, t_own, received, ()))
    total = call(total_kernel, shape((BLK, SP + TP), F32), parts)
    total = lax.ppermute(total, AXES, [(b, a) for a, b in piece_moves()])
    grad_spatial, grad_temporal = call(
        final_kernel, [shape((9, BLK, BLK), F32), shape((3, BLK, BLK), F32)], total
    )
    m, m1, m2, m3 = time_mix(lefts[3], (before, act4, after))
    ms = [over_b(s, l + 1) for l, s in enumerate((m1, m2, m3))]
    grad_inputs = call(finish_kernel, narrow, cot, d, *ds)
    output = finish_after([x, m, *ms], (grad_inputs,))

    return (
        output.reshape(inputs.shape),
        grad_inputs.reshape(inputs.shape),
        grad_spatial,
        grad_temporal,
        totals[0, :BLK],
        totals[0, 64 : 64 + BLK],
    )


def solution(mesh):
    in_specs = (
        P("ch", "dt", None),
        P(None, "ch", "dt"),
        P(None, "ch", "dt"),
        P("ch"),
        P("ch"),
        P("ch", "dt", None),
    )
    out_specs = (
        P("ch", "dt", None),
        P("ch", "dt", None),
        P(None, "ch", "dt"),
        P(None, "ch", "dt"),
        P("ch"),
        P("ch"),
    )
    return jax.shard_map(body, mesh=mesh, in_specs=in_specs, out_specs=out_specs, check_vma=False)
```

```python
import jax
import jax.numpy as jnp
from jax import lax
from jax.experimental import pallas as pl
from jax.experimental.pallas import tpu as pltpu
from jax.sharding import PartitionSpec as P

C = 640
G = 32
W = 64
CELLS = 2304
FRAMES = 16
BLK = 40
MEMBERS = (C // G) * FRAMES * CELLS
TAPS = ((-1, -1), (-1, 0), (-1, 1), (0, -1), (0, 0), (0, 1), (1, -1), (1, 0), (1, 1))
SP = 384
TP = 128
BF = jnp.bfloat16
F32 = jnp.float32

AXES = ("dt", "ch")
CORES = [list(range(0, 16, 2)), list(range(1, 16, 2))]


def split(block):
    return (block >> 1) & 3, ((block >> 3) << 1) | (block & 1)


def join(a, b):
    return ((b >> 1) << 3) | (a << 1) | (b & 1)


def over_a(value, k):
    return lax.ppermute(value, "ch", [(i, i ^ (k << 1)) for i in range(16)])


def over_b(value, l):
    mask = join(0, l)
    return lax.ppermute(value, "ch", [(i, i ^ mask) for i in range(16)])


def piece_moves():
    moves = []
    for into in range(16):
        for out in range(16):
            (a, b), (c, d) = split(into), split(out)
            place = ((a ^ c) * 4 + (b ^ d)) * 16 + join(c, b)
            moves.append((out * 16 + into, place))
    return moves


def neighbours(value):
    before = lax.ppermute(value, "dt", [(i, i + 1) for i in range(15)])
    after = lax.ppermute(value, "dt", [(i + 1, i) for i in range(15)])
    return before, after


def exchange(value):
    return lax.all_to_all(value, "dt", 0, 0)


def exchange8(value):
    return lax.all_to_all(value, "dt", 0, 0, axis_index_groups=CORES)


def other_core(value):
    return lax.ppermute(value, "dt", [(i, i ^ 1) for i in range(16)])


def params(limit=50):
    return pltpu.CompilerParams(vmem_limit_bytes=limit * 1024 * 1024)


def cost(micros=0):
    return pl.CostEstimate(flops=0, bytes_accessed=max(1, micros * 3000000), transcendentals=0)


def shape(dims, dtype):
    return jax.ShapeDtypeStruct(dims, dtype)


def shifted(value, row_step, col_step):
    cell = lax.broadcasted_iota(jnp.int32, (1, CELLS), 1)
    col = cell & (W - 1)
    inside = jnp.ones((1, CELLS), F32)
    if row_step == -1:
        inside = jnp.where(cell >= W, inside, 0.0)
    if row_step == 1:
        inside = jnp.where(cell < CELLS - W, inside, 0.0)
    if col_step == -1:
        inside = jnp.where(col >= 1, inside, 0.0)
    if col_step == 1:
        inside = jnp.where(col < W - 1, inside, 0.0)
    step = row_step * W + col_step
    if step == 0:
        return value
    return pltpu.roll(value, (-step) % CELLS, 1) * inside


def fill_taps(taps_ref, base, value, direction):
    wide = value.astype(F32)
    held = []
    for t, (a, b) in enumerate(TAPS):
        held.append(shifted(wide, direction * a, direction * b))
        if len(held) == 2:
            taps_ref[pl.ds(base + (t - 1) * BLK, 2 * BLK), :] = jnp.concatenate(held, 0).astype(BF)
            held = []
    held.append(jnp.zeros((SP - 9 * BLK, CELLS), F32))
    taps_ref[pl.ds(base + 8 * BLK, SP - 8 * BLK), :] = jnp.concatenate(held, 0).astype(BF)


class Pieces:
    def __init__(self, core, own, other):
        self.keep = 1.0 - core[0].astype(F32)
        self.refs = own, other

    def get(self, k, l, first, width):
        n = k * 4 + l
        own, other = [ref[n >> 1, :, first : first + width].astype(F32) for ref in self.refs]
        if n & 1:
            own, other = other, own
        return own * self.keep + other * (1.0 - self.keep)


def left_matrix(pieces, flipped, first, width):
    rows = []
    for r in range(4):
        parts = []
        for c in range(4):
            if flipped:
                turned = pieces.get(c, r, first, width).T
                count = width // BLK
                blocks = [turned[t * BLK : (t + 1) * BLK] for t in range(count)]
                blocks.append(jnp.zeros((BLK, width - count * BLK), F32))
                parts.append(jnp.concatenate(blocks, 1))
            else:
                parts.append(pieces.get(r, c, first, width))
        rows.append(jnp.concatenate(parts, 1))
    return jnp.concatenate(rows, 0).astype(BF)


def spread(left, right_ref, own_ref, send_refs):
    width = 256

    def chunk(c, carry):
        cols = pl.ds(pl.multiple_of(c * width, width), width)
        part = jnp.dot(left, right_ref[:, cols], preferred_element_type=F32)
        own_ref[:, cols] = part[:BLK]
        for n, ref in enumerate(send_refs):
            ref[:, cols] = part[(n + 1) * BLK : (n + 2) * BLK].astype(BF)
        return carry

    lax.fori_loop(0, CELLS // width, chunk, 0)


PARTIALS = [shape((BLK, CELLS), F32)] + [shape((BLK, CELLS), BF)] * 3


VMEM = pl.BlockSpec(memory_space=pltpu.VMEM)
SMEM = pl.BlockSpec(memory_space=pltpu.SMEM)
HBM = pl.BlockSpec(memory_space=pl.ANY)


def left_kernel(core, w_own, w_other, first, second, third, fourth):
    pieces = Pieces(core, w_own, w_other)
    first[...] = left_matrix(pieces, True, 0, SP)
    second[...] = left_matrix(pieces, False, 0, SP)
    third[...] = left_matrix(pieces, False, SP, TP)
    fourth[...] = left_matrix(pieces, True, SP, TP)


def left_matrices(core, w_own, w_other):
    return pl.pallas_call(
        left_kernel,
        out_shape=[shape((4 * BLK, 4 * width), BF) for width in (SP, SP, TP, TP)],
        in_specs=[SMEM] + [VMEM] * 2,
        compiler_params=params(),
        cost_estimate=cost(),
        name="left_matrices",
    )(core, w_own, w_other)


def conv_kernel(left, x0, x1, x2, x3, own, s1, s2, s3, taps):
    for k, ref in enumerate((x0, x1, x2, x3)):
        fill_taps(taps, k * SP, ref[...], 1)
    spread(left[...], taps, own, (s1, s2, s3))


def conv_forward(xs, left):
    return pl.pallas_call(
        conv_kernel,
        out_shape=PARTIALS,
        in_specs=[VMEM] * 5,
        scratch_shapes=[pltpu.VMEM((4 * SP, CELLS), BF)],
        compiler_params=params(),
        cost_estimate=cost(),
        name="conv_forward",
    )(left, *xs)


def back_kernel(*refs):
    core, left = refs[:2]
    gs, xs = refs[2:6], refs[6:10]
    own, s1, s2, s3, grad, grad_other, taps = refs[-7:]
    for l in range(4):
        fill_taps(taps, l * SP, gs[l][...], -1)
    spread(left[...], taps, own, (s1, s2, s3))
    field = jnp.concatenate([ref[...].astype(F32) for ref in xs], 0).astype(BF)
    products = [
        lax.dot_general(
            field, taps[l * SP : (l + 1) * SP, :], (((1,), (1,)), ((), ())), preferred_element_type=F32
        )
        for l in range(4)
    ]
    put_pieces(core, products, grad, grad_other, 0, SP)


def put_pieces(core, products, own, other, first, width):
    keep = 1.0 - core[0].astype(F32)
    for k in range(4):
        for l in (0, 2):
            even = products[l][k * BLK : (k + 1) * BLK]
            odd = products[l + 1][k * BLK : (k + 1) * BLK]
            n = (k * 4 + l) >> 1
            own[n, :, first : first + width] = even * keep + odd * (1.0 - keep)
            other[n, :, first : first + width] = even * (1.0 - keep) + odd * keep


def conv_backward(core, left, gs, xs):
    return pl.pallas_call(
        back_kernel,
        out_shape=PARTIALS + [shape((8, BLK, SP), F32)] * 2,
        in_specs=[SMEM] + [VMEM] * 9,
        out_specs=[VMEM] * 6,
        scratch_shapes=[pltpu.VMEM((4 * SP, CELLS), BF)],
        compiler_params=params(),
        cost_estimate=cost(),
        name="conv_backward",
    )(core, left, *gs, *xs)


def fill_frames(stack_ref, frames):
    for n in range(4):
        parts = [ref[n].astype(F32) for ref in frames]
        parts.append(jnp.zeros((TP - 3 * BLK, CELLS), F32))
        stack_ref[n * TP : (n + 1) * TP, :] = jnp.concatenate(parts, 0).astype(BF)


def time_mix_kernel(left, first, second, third, own, s1, s2, s3, stack):
    fill_frames(stack, (first, second, third))
    spread(left[...], stack, own, (s1, s2, s3))


def time_mix(left, frames):
    return pl.pallas_call(
        time_mix_kernel,
        out_shape=PARTIALS,
        in_specs=[VMEM] * 4,
        scratch_shapes=[pltpu.VMEM((4 * TP, CELLS), BF)],
        compiler_params=params(),
        cost_estimate=cost(),
        name="time_mix",
    )(left, *frames)


def time_grad_kernel(core, act, first, second, third, grad, grad_other, stack):
    fill_frames(stack, (first, second, third))
    field = jnp.concatenate([act[k].astype(F32) for k in range(4)], 0).astype(BF)
    part = lax.dot_general(field, stack[...], (((1,), (1,)), ((), ())), preferred_element_type=F32)
    products = [part[:, l * TP : (l + 1) * TP] for l in range(4)]
    put_pieces(core, products, grad, grad_other, 0, TP)


def time_grad(core, act4, frames):
    return pl.pallas_call(
        time_grad_kernel,
        out_shape=[shape((8, BLK, TP), F32)] * 2,
        in_specs=[SMEM] + [VMEM] * 4,
        scratch_shapes=[pltpu.VMEM((4 * TP, CELLS), BF)],
        compiler_params=params(),
        cost_estimate=cost(),
        name="time_grad",
    )(core, act4, *frames)


def hold_kernel(value, *refs):
    refs[-1][...] = value[...]


def hold_after(value, after):
    return pl.pallas_call(
        hold_kernel,
        out_shape=shape(value.shape, value.dtype),
        in_specs=[VMEM] + [HBM] * len(after),
        compiler_params=params(),
        cost_estimate=cost(),
        name="hold_after",
    )(value, *after)


def stack_kernel(p0, p1, p2, p3, *refs):
    for n, ref in enumerate((p0, p1, p2, p3)):
        refs[-1][n] = ref[...]


def stack_after(parts, after):
    return pl.pallas_call(
        stack_kernel,
        out_shape=shape((4, BLK, CELLS), BF),
        in_specs=[VMEM] * 4 + [HBM] * len(after),
        compiler_params=params(),
        cost_estimate=cost(),
        name="stack_after",
    )(*parts, *after)


def merge_kernel(spatial, temporal, out):
    out[:, :, 0:SP] = spatial[...]
    out[:, :, SP:] = temporal[...]


def pair_kernel(s0, t0, received, *refs):
    out = refs[-1]
    out[:, :, 0:SP] = (s0[...] + received[:, :, 0:SP]).astype(BF)
    out[:, :, SP:] = (t0[...] + received[:, :, SP:]).astype(BF)


def pair_sum(s0, t0, received, after):
    return pl.pallas_call(
        pair_kernel,
        out_shape=shape((8, BLK, SP + TP), BF),
        in_specs=[VMEM] * 3 + [HBM] * len(after),
        compiler_params=params(),
        cost_estimate=cost(),
        name="pair_sum",
    )(s0, t0, received, *after)


def prepare_kernel(spatial, temporal, out):
    def row(pieces, width):
        filler = jnp.zeros((BLK, width - len(pieces) * BLK), F32)
        return jnp.concatenate(pieces + [filler], 1)

    first = [spatial[t].astype(F32) for t in range(9)]
    second = [temporal[t].astype(F32) for t in range(3)]
    out[...] = jnp.concatenate([row(first, SP), row(second, TP)], 1).astype(BF)


def add_up(own, r1, r2, r3):
    return own[...] + r1[...].astype(F32) + r2[...].astype(F32) + r3[...].astype(F32)


def lane_rows():
    return (
        lax.broadcasted_iota(jnp.int32, (BLK, 128), 0),
        lax.broadcasted_iota(jnp.int32, (BLK, 128), 1),
    )


def to_lanes(low, high):
    row, lane = lane_rows()
    both = jnp.where(lane == row, low, 0.0) + jnp.where(lane == row + 64, high, 0.0)
    return jnp.sum(both, axis=0, keepdims=True)


def column(row_ref):
    row = lax.broadcasted_iota(jnp.int32, (BLK, BLK), 0)
    lane = lax.broadcasted_iota(jnp.int32, (BLK, BLK), 1)
    return jnp.sum(jnp.where(row == lane, row_ref[...], 0.0), axis=1, keepdims=True)


def group_sum(values):
    row = lax.broadcasted_iota(jnp.int32, (BLK, 1), 0)
    low = jnp.sum(jnp.where(row < BLK // 2, values, 0.0), axis=0, keepdims=True)
    high = jnp.sum(jnp.where(row < BLK // 2, 0.0, values), axis=0, keepdims=True)
    return jnp.where(row < BLK // 2, low, high)


def put_sums(sums, low, high):
    sums[...] = jnp.broadcast_to(to_lanes(low, high).reshape(1, 1, 128), (16, 1, 128))


def get_sums(sums):
    total = jnp.sum(sums[...], axis=0)
    row, lane = lane_rows()
    low = jnp.sum(jnp.where(lane == row, total, 0.0), axis=1, keepdims=True)
    high = jnp.sum(jnp.where(lane == row + 64, total, 0.0), axis=1, keepdims=True)
    return total, low, high


def stats_kernel(own, r1, r2, r3, conv, sums):
    rounded = add_up(own, r1, r2, r3).astype(BF)
    conv[...] = rounded
    wide = rounded.astype(F32)
    put_sums(
        sums, jnp.sum(wide, axis=1, keepdims=True), jnp.sum(wide * wide, axis=1, keepdims=True)
    )


def act_kernel(conv, sums, gain, bias, u0, u1, u2, u3, act, normed, grad_affine, inv, sums2):
    _, low, high = get_sums(sums)
    center = group_sum(low) / MEMBERS
    inverse = lax.rsqrt(group_sum(high) / MEMBERS - center * center + 1e-05)
    inv[...] = jnp.broadcast_to(inverse, (BLK, 128))
    norm = (conv[...].astype(F32) - center) * inverse
    normed[...] = norm
    affine = norm * column(gain) + column(bias)
    sigmoid = jax.nn.sigmoid(affine)
    act[...] = (affine * sigmoid).astype(BF)
    grad = add_up(u0, u1, u2, u3) * sigmoid * (1.0 + affine * (1.0 - sigmoid))
    grad_affine[...] = grad
    put_sums(
        sums2, jnp.sum(grad * norm, axis=1, keepdims=True), jnp.sum(grad, axis=1, keepdims=True)
    )


def grad_kernel(normed, grad_affine, inv, sums2, gain, grad_conv, totals):
    total, gain_sum, bias_sum = get_sums(sums2)
    totals[...] = total
    scale = column(gain)
    first = group_sum(scale * bias_sum) / MEMBERS
    second = group_sum(scale * gain_sum) / MEMBERS
    value = inv[:, 0:1] * (grad_affine[...] * scale - first - normed[...] * second)
    grad_conv[...] = value.astype(BF)


def finish_kernel(start, own, r1, r2, r3, *refs):
    refs[-1][...] = (start[...].astype(F32) + add_up(own, r1, r2, r3)).astype(BF)


def finish_after(values, after):
    return pl.pallas_call(
        finish_kernel,
        out_shape=shape((BLK, CELLS), BF),
        in_specs=[VMEM] * 5 + [HBM] * len(after),
        compiler_params=params(),
        cost_estimate=cost(),
        name="finish_after",
    )(*values, *after)


def total_kernel(parts, total):
    total[...] = jnp.sum(parts[...].astype(F32), axis=0)


def final_kernel(total, spatial, temporal):
    value = total[...]
    for t in range(9):
        spatial[t] = value[:, t * BLK : (t + 1) * BLK]
    for t in range(3):
        temporal[t] = value[:, SP + t * BLK : SP + (t + 1) * BLK]


def repeat_kernel(value, *refs):
    out = refs[-1]
    for n in range(8):
        out[n] = value[...]


def repeat_after(value, *after):
    vmem = pl.BlockSpec(memory_space=pltpu.VMEM)
    return pl.pallas_call(
        repeat_kernel,
        out_shape=shape((8,) + value.shape, value.dtype),
        in_specs=[vmem] + [pl.BlockSpec(memory_space=pl.ANY)] * len(after),
        out_specs=vmem,
        compiler_params=params(),
        cost_estimate=cost(),
        name="repeat_after",
    )(value, *after)


def call(kernel, outs, *args, limit=50, micros=0):
    return pl.pallas_call(
        kernel,
        out_shape=outs,
        compiler_params=params(limit),
        cost_estimate=cost(micros),
        name=kernel.__name__,
    )(*args)


def body(inputs, spatial_weight, temporal_weight, norm_gain, norm_bias, cotangent):
    wide = shape((BLK, CELLS), F32)
    narrow = shape((BLK, CELLS), BF)
    small = shape((16, 1, 128), F32)
    core = (lax.axis_index("dt") & 1).reshape(1)
    x, cot = inputs.reshape(BLK, CELLS), cotangent.reshape(BLK, CELLS)
    gain, bias = norm_gain.reshape(1, BLK), norm_bias.reshape(1, BLK)

    local = call(prepare_kernel, shape((BLK, SP + TP), BF), spatial_weight, temporal_weight)
    moved = lax.ppermute(local, AXES, piece_moves())
    xs = [x] + [over_a(x, k) for k in (1, 2, 3)]
    cots = [cot] + [over_b(cot, l) for l in (1, 2, 3)]
    w_own = exchange8(repeat_after(moved, xs[1], xs[3], cots[3]))
    lefts = left_matrices(core, w_own, other_core(w_own))

    cot4 = stack_after(cots, (moved,))
    cot_before, cot_after = neighbours(cot4)
    cot_frames = (cot_after, cot4, cot_before)

    own, s1, s2, s3 = conv_forward(xs, lefts[0])
    received = [over_b(s, l + 1) for l, s in enumerate((s1, s2, s3))]
    u, u1, u2, u3 = time_mix(lefts[2], cot_frames)
    us = [u] + [over_a(s, k + 1) for k, s in enumerate((u1, u2, u3))]

    conv, sums = call(stats_kernel, [narrow, small], own, *received)
    act, normed, grad_affine, inv, sums2 = call(
        act_kernel,
        [narrow, wide, wide, shape((BLK, 128), F32), small],
        conv, exchange(sums), gain, bias, *us,
    )
    acts = [act] + [over_a(act, k) for k in (1, 2, 3)]
    grad_conv, totals = call(
        grad_kernel,
        [narrow, shape((1, 128), F32)],
        normed, grad_affine, inv, exchange(sums2), gain,
    )
    gs = [grad_conv] + [over_b(grad_conv, l) for l in (1, 2, 3)]
    act4 = stack_after(acts, (grad_conv,))
    before, after = neighbours(act4)

    d, d1, d2, d3, s_own, s_other = conv_backward(core, lefts[1], gs, xs)
    ds = [over_a(s, k + 1) for k, s in enumerate((d1, d2, d3))]
    t_own, t_other = time_grad(core, act4, cot_frames)

    received = other_core(call(merge_kernel, shape((8, BLK, SP + TP), F32), s_other, t_other))
    parts = exchange8(pair_sum(s_own, t_own, received, ()))
    total = call(total_kernel, shape((BLK, SP + TP), F32), parts)
    total = lax.ppermute(total, AXES, [(b, a) for a, b in piece_moves()])
    grad_spatial, grad_temporal = call(
        final_kernel, [shape((9, BLK, BLK), F32), shape((3, BLK, BLK), F32)], total
    )
    m, m1, m2, m3 = time_mix(lefts[3], (before, act4, after))
    ms = [over_b(s, l + 1) for l, s in enumerate((m1, m2, m3))]
    grad_inputs = call(finish_kernel, narrow, cot, d, *ds)
    output = finish_after([x, m, *ms], (grad_inputs,))

    return (
        output.reshape(inputs.shape),
        grad_inputs.reshape(inputs.shape),
        grad_spatial,
        grad_temporal,
        totals[0, :BLK],
        totals[0, 64 : 64 + BLK],
    )


def solution(mesh):
    in_specs = (
        P("ch", "dt", None),
        P(None, "ch", "dt"),
        P(None, "ch", "dt"),
        P("ch"),
        P("ch"),
        P("ch", "dt", None),
    )
    out_specs = (
        P("ch", "dt", None),
        P("ch", "dt", None),
        P(None, "ch", "dt"),
        P(None, "ch", "dt"),
        P("ch"),
        P("ch"),
    )
    return jax.shard_map(body, mesh=mesh, in_specs=in_specs, out_specs=out_specs, check_vma=False)
```

```python
import jax
import jax.numpy as jnp
from jax import lax
from jax.experimental import pallas as pl
from jax.experimental.pallas import tpu as pltpu
from jax.sharding import PartitionSpec as P

C = 640
G = 32
W = 64
CELLS = 2304
FRAMES = 16
BLK = 40
MEMBERS = (C // G) * FRAMES * CELLS
TAPS = ((-1, -1), (-1, 0), (-1, 1), (0, -1), (0, 0), (0, 1), (1, -1), (1, 0), (1, 1))
SP = 384
TP = 128
BF = jnp.bfloat16
F32 = jnp.float32

AXES = ("dt", "ch")
CORES = [list(range(0, 16, 2)), list(range(1, 16, 2))]


def split(block):
    return (block >> 1) & 3, ((block >> 3) << 1) | (block & 1)


def join(a, b):
    return ((b >> 1) << 3) | (a << 1) | (b & 1)


def over_a(value, k):
    return lax.ppermute(value, "ch", [(i, i ^ (k << 1)) for i in range(16)])


def over_b(value, l):
    mask = join(0, l)
    return lax.ppermute(value, "ch", [(i, i ^ mask) for i in range(16)])


def piece_moves():
    moves = []
    for into in range(16):
        for out in range(16):
            (a, b), (c, d) = split(into), split(out)
            place = ((a ^ c) * 4 + (b ^ d)) * 16 + join(c, b)
            moves.append((out * 16 + into, place))
    return moves


def neighbours(value):
    before = lax.ppermute(value, "dt", [(i, i + 1) for i in range(15)])
    after = lax.ppermute(value, "dt", [(i + 1, i) for i in range(15)])
    return before, after


def exchange(value):
    return lax.all_to_all(value, "dt", 0, 0)


def exchange8(value):
    return lax.all_to_all(value, "dt", 0, 0, axis_index_groups=CORES)


def other_core(value):
    return lax.ppermute(value, "dt", [(i, i ^ 1) for i in range(16)])


def params(limit=50):
    return pltpu.CompilerParams(vmem_limit_bytes=limit * 1024 * 1024)


def cost(micros=0):
    return pl.CostEstimate(flops=0, bytes_accessed=max(1, micros * 3000000), transcendentals=0)


def shape(dims, dtype):
    return jax.ShapeDtypeStruct(dims, dtype)


def shifted(value, row_step, col_step):
    cell = lax.broadcasted_iota(jnp.int32, (1, CELLS), 1)
    col = cell & (W - 1)
    inside = jnp.ones((1, CELLS), F32)
    if row_step == -1:
        inside = jnp.where(cell >= W, inside, 0.0)
    if row_step == 1:
        inside = jnp.where(cell < CELLS - W, inside, 0.0)
    if col_step == -1:
        inside = jnp.where(col >= 1, inside, 0.0)
    if col_step == 1:
        inside = jnp.where(col < W - 1, inside, 0.0)
    step = row_step * W + col_step
    if step == 0:
        return value
    return pltpu.roll(value, (-step) % CELLS, 1) * inside


def fill_taps(taps_ref, base, value, direction):
    wide = value.astype(F32)
    held = []
    for t, (a, b) in enumerate(TAPS):
        held.append(shifted(wide, direction * a, direction * b))
        if len(held) == 2:
            taps_ref[pl.ds(base + (t - 1) * BLK, 2 * BLK), :] = jnp.concatenate(held, 0).astype(BF)
            held = []
    held.append(jnp.zeros((SP - 9 * BLK, CELLS), F32))
    taps_ref[pl.ds(base + 8 * BLK, SP - 8 * BLK), :] = jnp.concatenate(held, 0).astype(BF)


class Pieces:
    def __init__(self, core, own, other):
        self.keep = 1.0 - core[0].astype(F32)
        self.refs = own, other

    def get(self, k, l, first, width):
        n = k * 4 + l
        own, other = [ref[n >> 1, :, first : first + width].astype(F32) for ref in self.refs]
        if n & 1:
            own, other = other, own
        return own * self.keep + other * (1.0 - self.keep)


def left_matrix(pieces, flipped, first, width):
    rows = []
    for r in range(4):
        parts = []
        for c in range(4):
            if flipped:
                turned = pieces.get(c, r, first, width).T
                count = width // BLK
                blocks = [turned[t * BLK : (t + 1) * BLK] for t in range(count)]
                blocks.append(jnp.zeros((BLK, width - count * BLK), F32))
                parts.append(jnp.concatenate(blocks, 1))
            else:
                parts.append(pieces.get(r, c, first, width))
        rows.append(jnp.concatenate(parts, 1))
    return jnp.concatenate(rows, 0).astype(BF)


def spread(left, right_ref, own_ref, send_refs):
    width = 256

    def chunk(c, carry):
        cols = pl.ds(pl.multiple_of(c * width, width), width)
        part = jnp.dot(left, right_ref[:, cols], preferred_element_type=F32)
        own_ref[:, cols] = part[:BLK]
        for n, ref in enumerate(send_refs):
            ref[:, cols] = part[(n + 1) * BLK : (n + 2) * BLK].astype(BF)
        return carry

    lax.fori_loop(0, CELLS // width, chunk, 0)


PARTIALS = [shape((BLK, CELLS), F32)] + [shape((BLK, CELLS), BF)] * 3


VMEM = pl.BlockSpec(memory_space=pltpu.VMEM)
SMEM = pl.BlockSpec(memory_space=pltpu.SMEM)
HBM = pl.BlockSpec(memory_space=pl.ANY)


def left_kernel(core, w_own, w_other, first, second, third, fourth):
    pieces = Pieces(core, w_own, w_other)
    first[...] = left_matrix(pieces, True, 0, SP)
    second[...] = left_matrix(pieces, False, 0, SP)
    third[...] = left_matrix(pieces, False, SP, TP)
    fourth[...] = left_matrix(pieces, True, SP, TP)


def left_matrices(core, w_own, w_other):
    return pl.pallas_call(
        left_kernel,
        out_shape=[shape((4 * BLK, 4 * width), BF) for width in (SP, SP, TP, TP)],
        in_specs=[SMEM] + [VMEM] * 2,
        compiler_params=params(),
        cost_estimate=cost(),
        name="left_matrices",
    )(core, w_own, w_other)


def conv_kernel(left, x0, x1, x2, x3, own, s1, s2, s3, taps):
    for k, ref in enumerate((x0, x1, x2, x3)):
        fill_taps(taps, k * SP, ref[...], 1)
    spread(left[...], taps, own, (s1, s2, s3))


def conv_forward(xs, left):
    return pl.pallas_call(
        conv_kernel,
        out_shape=PARTIALS,
        in_specs=[VMEM] * 5,
        scratch_shapes=[pltpu.VMEM((4 * SP, CELLS), BF)],
        compiler_params=params(),
        cost_estimate=cost(),
        name="conv_forward",
    )(left, *xs)


def back_kernel(*refs):
    core, left = refs[:2]
    gs, xs = refs[2:6], refs[6:10]
    own, s1, s2, s3, grad, grad_other, taps = refs[-7:]
    for l in range(4):
        fill_taps(taps, l * SP, gs[l][...], -1)
    spread(left[...], taps, own, (s1, s2, s3))
    field = jnp.concatenate([ref[...].astype(F32) for ref in xs], 0).astype(BF)
    products = [
        lax.dot_general(
            field, taps[l * SP : (l + 1) * SP, :], (((1,), (1,)), ((), ())), preferred_element_type=F32
        )
        for l in range(4)
    ]
    put_pieces(core, products, grad, grad_other, 0, SP)


def put_pieces(core, products, own, other, first, width):
    keep = 1.0 - core[0].astype(F32)
    for k in range(4):
        for l in (0, 2):
            even = products[l][k * BLK : (k + 1) * BLK]
            odd = products[l + 1][k * BLK : (k + 1) * BLK]
            n = (k * 4 + l) >> 1
            own[n, :, first : first + width] = even * keep + odd * (1.0 - keep)
            other[n, :, first : first + width] = even * (1.0 - keep) + odd * keep


def conv_backward(core, left, gs, xs):
    return pl.pallas_call(
        back_kernel,
        out_shape=PARTIALS + [shape((8, BLK, SP), F32)] * 2,
        in_specs=[SMEM] + [VMEM] * 9,
        out_specs=[VMEM] * 6,
        scratch_shapes=[pltpu.VMEM((4 * SP, CELLS), BF)],
        compiler_params=params(),
        cost_estimate=cost(),
        name="conv_backward",
    )(core, left, *gs, *xs)


def fill_frames(stack_ref, frames):
    for n in range(4):
        parts = [ref[n].astype(F32) for ref in frames]
        parts.append(jnp.zeros((TP - 3 * BLK, CELLS), F32))
        stack_ref[n * TP : (n + 1) * TP, :] = jnp.concatenate(parts, 0).astype(BF)


def time_mix_kernel(left, first, second, third, own, s1, s2, s3, stack):
    fill_frames(stack, (first, second, third))
    spread(left[...], stack, own, (s1, s2, s3))


def time_mix(left, frames):
    return pl.pallas_call(
        time_mix_kernel,
        out_shape=PARTIALS,
        in_specs=[VMEM] * 4,
        scratch_shapes=[pltpu.VMEM((4 * TP, CELLS), BF)],
        compiler_params=params(),
        cost_estimate=cost(),
        name="time_mix",
    )(left, *frames)


def time_grad_kernel(core, act, first, second, third, grad, grad_other, stack):
    fill_frames(stack, (first, second, third))
    field = jnp.concatenate([act[k].astype(F32) for k in range(4)], 0).astype(BF)
    part = lax.dot_general(field, stack[...], (((1,), (1,)), ((), ())), preferred_element_type=F32)
    products = [part[:, l * TP : (l + 1) * TP] for l in range(4)]
    put_pieces(core, products, grad, grad_other, 0, TP)


def time_grad(core, act4, frames):
    return pl.pallas_call(
        time_grad_kernel,
        out_shape=[shape((8, BLK, TP), F32)] * 2,
        in_specs=[SMEM] + [VMEM] * 4,
        scratch_shapes=[pltpu.VMEM((4 * TP, CELLS), BF)],
        compiler_params=params(),
        cost_estimate=cost(),
        name="time_grad",
    )(core, act4, *frames)


def hold_kernel(value, *refs):
    refs[-1][...] = value[...]


def hold_after(value, after):
    return pl.pallas_call(
        hold_kernel,
        out_shape=shape(value.shape, value.dtype),
        in_specs=[VMEM] + [HBM] * len(after),
        compiler_params=params(),
        cost_estimate=cost(),
        name="hold_after",
    )(value, *after)


def stack_kernel(p0, p1, p2, p3, *refs):
    for n, ref in enumerate((p0, p1, p2, p3)):
        refs[-1][n] = ref[...]


def stack_after(parts, after):
    return pl.pallas_call(
        stack_kernel,
        out_shape=shape((4, BLK, CELLS), BF),
        in_specs=[VMEM] * 4 + [HBM] * len(after),
        compiler_params=params(),
        cost_estimate=cost(),
        name="stack_after",
    )(*parts, *after)


def merge_kernel(spatial, temporal, out):
    out[:, :, 0:SP] = spatial[...]
    out[:, :, SP:] = temporal[...]


def pair_kernel(s0, t0, received, *refs):
    out = refs[-1]
    out[:, :, 0:SP] = (s0[...] + received[:, :, 0:SP]).astype(BF)
    out[:, :, SP:] = (t0[...] + received[:, :, SP:]).astype(BF)


def pair_sum(s0, t0, received, after):
    return pl.pallas_call(
        pair_kernel,
        out_shape=shape((8, BLK, SP + TP), BF),
        in_specs=[VMEM] * 3 + [HBM] * len(after),
        compiler_params=params(),
        cost_estimate=cost(),
        name="pair_sum",
    )(s0, t0, received, *after)


def prepare_kernel(spatial, temporal, out):
    def row(pieces, width):
        filler = jnp.zeros((BLK, width - len(pieces) * BLK), F32)
        return jnp.concatenate(pieces + [filler], 1)

    first = [spatial[t].astype(F32) for t in range(9)]
    second = [temporal[t].astype(F32) for t in range(3)]
    out[...] = jnp.concatenate([row(first, SP), row(second, TP)], 1).astype(BF)


def add_up(own, r1, r2, r3):
    return own[...] + r1[...].astype(F32) + r2[...].astype(F32) + r3[...].astype(F32)


def lane_rows():
    return (
        lax.broadcasted_iota(jnp.int32, (BLK, 128), 0),
        lax.broadcasted_iota(jnp.int32, (BLK, 128), 1),
    )


def to_lanes(low, high):
    row, lane = lane_rows()
    both = jnp.where(lane == row, low, 0.0) + jnp.where(lane == row + 64, high, 0.0)
    return jnp.sum(both, axis=0, keepdims=True)


def column(row_ref):
    row = lax.broadcasted_iota(jnp.int32, (BLK, BLK), 0)
    lane = lax.broadcasted_iota(jnp.int32, (BLK, BLK), 1)
    return jnp.sum(jnp.where(row == lane, row_ref[...], 0.0), axis=1, keepdims=True)


def group_sum(values):
    row = lax.broadcasted_iota(jnp.int32, (BLK, 1), 0)
    low = jnp.sum(jnp.where(row < BLK // 2, values, 0.0), axis=0, keepdims=True)
    high = jnp.sum(jnp.where(row < BLK // 2, 0.0, values), axis=0, keepdims=True)
    return jnp.where(row < BLK // 2, low, high)


def put_sums(sums, low, high):
    sums[...] = jnp.broadcast_to(to_lanes(low, high).reshape(1, 1, 128), (16, 1, 128))


def get_sums(sums):
    total = jnp.sum(sums[...], axis=0)
    row, lane = lane_rows()
    low = jnp.sum(jnp.where(lane == row, total, 0.0), axis=1, keepdims=True)
    high = jnp.sum(jnp.where(lane == row + 64, total, 0.0), axis=1, keepdims=True)
    return total, low, high


def stats_kernel(own, r1, r2, r3, conv, sums):
    rounded = add_up(own, r1, r2, r3).astype(BF)
    conv[...] = rounded
    wide = rounded.astype(F32)
    put_sums(
        sums, jnp.sum(wide, axis=1, keepdims=True), jnp.sum(wide * wide, axis=1, keepdims=True)
    )


def act_kernel(conv, sums, gain, bias, u0, u1, u2, u3, act, normed, grad_affine, inv, sums2):
    _, low, high = get_sums(sums)
    center = group_sum(low) / MEMBERS
    inverse = lax.rsqrt(group_sum(high) / MEMBERS - center * center + 1e-05)
    inv[...] = jnp.broadcast_to(inverse, (BLK, 128))
    norm = (conv[...].astype(F32) - center) * inverse
    normed[...] = norm
    affine = norm * column(gain) + column(bias)
    sigmoid = jax.nn.sigmoid(affine)
    act[...] = (affine * sigmoid).astype(BF)
    grad = add_up(u0, u1, u2, u3) * sigmoid * (1.0 + affine * (1.0 - sigmoid))
    grad_affine[...] = grad
    put_sums(
        sums2, jnp.sum(grad * norm, axis=1, keepdims=True), jnp.sum(grad, axis=1, keepdims=True)
    )


def grad_kernel(normed, grad_affine, inv, sums2, gain, grad_conv, totals):
    total, gain_sum, bias_sum = get_sums(sums2)
    totals[...] = total
    scale = column(gain)
    first = group_sum(scale * bias_sum) / MEMBERS
    second = group_sum(scale * gain_sum) / MEMBERS
    value = inv[:, 0:1] * (grad_affine[...] * scale - first - normed[...] * second)
    grad_conv[...] = value.astype(BF)


def finish_kernel(start, own, r1, r2, r3, *refs):
    refs[-1][...] = (start[...].astype(F32) + add_up(own, r1, r2, r3)).astype(BF)


def finish_after(values, after):
    return pl.pallas_call(
        finish_kernel,
        out_shape=shape((BLK, CELLS), BF),
        in_specs=[VMEM] * 5 + [HBM] * len(after),
        compiler_params=params(),
        cost_estimate=cost(),
        name="finish_after",
    )(*values, *after)


def total_kernel(parts, total):
    total[...] = jnp.sum(parts[...].astype(F32), axis=0)


def final_kernel(total, spatial, temporal):
    value = total[...]
    for t in range(9):
        spatial[t] = value[:, t * BLK : (t + 1) * BLK]
    for t in range(3):
        temporal[t] = value[:, SP + t * BLK : SP + (t + 1) * BLK]


def repeat_kernel(value, *refs):
    out = refs[-1]
    for n in range(8):
        out[n] = value[...]


def repeat_after(value, *after):
    vmem = pl.BlockSpec(memory_space=pltpu.VMEM)
    return pl.pallas_call(
        repeat_kernel,
        out_shape=shape((8,) + value.shape, value.dtype),
        in_specs=[vmem] + [pl.BlockSpec(memory_space=pl.ANY)] * len(after),
        out_specs=vmem,
        compiler_params=params(),
        cost_estimate=cost(),
        name="repeat_after",
    )(value, *after)


def call(kernel, outs, *args, limit=50, micros=0):
    return pl.pallas_call(
        kernel,
        out_shape=outs,
        compiler_params=params(limit),
        cost_estimate=cost(micros),
        name=kernel.__name__,
    )(*args)


def body(inputs, spatial_weight, temporal_weight, norm_gain, norm_bias, cotangent):
    wide = shape((BLK, CELLS), F32)
    narrow = shape((BLK, CELLS), BF)
    small = shape((16, 1, 128), F32)
    core = (lax.axis_index("dt") & 1).reshape(1)
    x, cot = inputs.reshape(BLK, CELLS), cotangent.reshape(BLK, CELLS)
    gain, bias = norm_gain.reshape(1, BLK), norm_bias.reshape(1, BLK)

    local = call(prepare_kernel, shape((BLK, SP + TP), BF), spatial_weight, temporal_weight)
    moved = lax.ppermute(local, AXES, piece_moves())
    xs = [x] + [over_a(x, k) for k in (1, 2, 3)]
    cots = [cot] + [over_b(cot, l) for l in (1, 2, 3)]
    w_own = exchange8(repeat_after(moved, *xs[1:]))
    lefts = left_matrices(core, w_own, other_core(w_own))

    cot4 = stack_after(cots, (moved,))
    cot_before, cot_after = neighbours(cot4)
    cot_frames = (cot_after, cot4, cot_before)

    own, s1, s2, s3 = conv_forward(xs, lefts[0])
    received = [over_b(s, l + 1) for l, s in enumerate((s1, s2, s3))]
    u, u1, u2, u3 = time_mix(lefts[2], cot_frames)
    us = [u] + [over_a(s, k + 1) for k, s in enumerate((u1, u2, u3))]

    conv, sums = call(stats_kernel, [narrow, small], own, *received)
    act, normed, grad_affine, inv, sums2 = call(
        act_kernel,
        [narrow, wide, wide, shape((BLK, 128), F32), small],
        conv, exchange(sums), gain, bias, *us,
    )
    acts = [act] + [over_a(act, k) for k in (1, 2, 3)]
    grad_conv, totals = call(
        grad_kernel,
        [narrow, shape((1, 128), F32)],
        normed, grad_affine, inv, exchange(sums2), gain,
    )
    gs = [grad_conv] + [over_b(grad_conv, l) for l in (1, 2, 3)]
    act4 = stack_after(acts, (grad_conv,))
    before, after = neighbours(act4)

    d, d1, d2, d3, s_own, s_other = conv_backward(core, lefts[1], gs, xs)
    ds = [over_a(s, k + 1) for k, s in enumerate((d1, d2, d3))]
    t_own, t_other = time_grad(core, act4, cot_frames)

    received = other_core(call(merge_kernel, shape((8, BLK, SP + TP), F32), s_other, t_other))
    parts = exchange8(pair_sum(s_own, t_own, received, ()))
    total = call(total_kernel, shape((BLK, SP + TP), F32), parts)
    total = lax.ppermute(total, AXES, [(b, a) for a, b in piece_moves()])
    grad_spatial, grad_temporal = call(
        final_kernel, [shape((9, BLK, BLK), F32), shape((3, BLK, BLK), F32)], total
    )
    m, m1, m2, m3 = time_mix(lefts[3], (before, act4, after))
    ms = [over_b(s, l + 1) for l, s in enumerate((m1, m2, m3))]
    grad_inputs = call(finish_kernel, narrow, cot, d, *ds)
    output = finish_after([x, m, *ms], (grad_inputs,))

    return (
        output.reshape(inputs.shape),
        grad_inputs.reshape(inputs.shape),
        grad_spatial,
        grad_temporal,
        totals[0, :BLK],
        totals[0, 64 : 64 + BLK],
    )


def solution(mesh):
    in_specs = (
        P("ch", "dt", None),
        P(None, "ch", "dt"),
        P(None, "ch", "dt"),
        P("ch"),
        P("ch"),
        P("ch", "dt", None),
    )
    out_specs = (
        P("ch", "dt", None),
        P("ch", "dt", None),
        P(None, "ch", "dt"),
        P(None, "ch", "dt"),
        P("ch"),
        P("ch"),
    )
    return jax.shard_map(body, mesh=mesh, in_specs=in_specs, out_specs=out_specs, check_vma=False)
```
